128 devices in a mesh: head: 8 (over x, y_lo), blk: 16 (over y_hi, z, core).
Axes of the slice: x: 4, y: 4 (y_hi: 2, y_lo: 2; y = y_hi * 2 + y_lo), z: 4, core: 2. Of those that a mesh axis runs over, the one named last changes fastest.
Arguments:
- tokens: bfloat16 [8, 2048, 2048], P('head', 'blk'), may hold values from -6 to 6
- block_lengths: int32 [8, 12], replicated, may hold values from 1 to 256, 2048 in all within a row
- attn_gain: float32 [2048], replicated, may hold values from 0.1 to 1.9
- query_weight: bfloat16 [2048, 2048], P('blk', 'head'), may hold values from -0.125 to 0.125
- key_weight: bfloat16 [2048, 2048], P('blk', 'head'), may hold values from -0.125 to 0.125
- value_weight: bfloat16 [2048, 2048], P('blk', 'head'), may hold values from -0.125 to 0.125
- out_weight: bfloat16 [2048, 2048], P('head', 'blk'), may hold values from -2 to 2
- mlp_gain: float32 [2048], replicated, may hold values from 0.1 to 1.9
- gate_weight: bfloat16 [2048, 5504], P('blk', 'head'), may hold values from -0.125 to 0.125
- up_weight: bfloat16 [2048, 5504], P('blk', 'head'), may hold values from -0.125 to 0.125
- down_weight: bfloat16 [5504, 2048], P('head', 'blk'), may hold values from -0.078125 to 0.078125
- output_grad: bfloat16 [8, 2048, 2048], P('head', 'blk'), may hold values from -6 to 6
Outputs:
- layer_output: bfloat16 [8, 2048, 2048], P('head', 'blk')
- input_grad: float32 [8, 2048, 2048], P('head', 'blk')
- attn_gain_grad: float32 [2048], replicated
- query_weight_grad: float32 [2048, 2048], P('blk', 'head')
- key_weight_grad: float32 [2048, 2048], P('blk', 'head')
- value_weight_grad: float32 [2048, 2048], P('blk', 'head')
- out_weight_grad: float32 [2048, 2048], P('head', 'blk')
- mlp_gain_grad: float32 [2048], replicated
- gate_weight_grad: float32 [2048, 5504], P('blk', 'head')
- up_weight_grad: float32 [2048, 5504], P('blk', 'head')
- down_weight_grad: float32 [5504, 2048], P('head', 'blk')
The draws below stay inside these ranges and needn't reach their ends.
Inputs may be any that keep to these rules, and one draw needn't show every extreme that they name: `block_lengths`: row s holds the token counts of the 12 consecutive attention blocks of sequence s, in order; each row sums to 2048 and its largest count is 256.
All inputs are finite; a program needn't handle non-finite values.
Results may differ from the reference program's by a relative error of at most 0.028.
Values may be sent and summed in bfloat16 or wider, within the bound.
No kernel may reach another device: no remote copies, remote signals or barrier semaphores. Data moves between devices by JAX's collectives and lax.ppermute only.
A program may use at most 128 MiB of HBM per device.

```python
import math
import jax
import jax.numpy as jnp
import numpy as np
from jax import lax

D = 2048
HEADS = 16
FF = 5504
HEAD_DIM = 128
SEQ = 2048
BLOCK_MOST = 256
BLOCKS = 12
SEQS = 8


def spiked(array, rng, source, target, blocks, factor):
    owner, partner = [(jnp.arange(array.shape[dim]) // (array.shape[dim] // blocks)).reshape([-1 if axis == dim else 1 for axis in range(array.ndim)]) for dim in (source, target)]
    chosen = jax.random.permutation(rng, blocks)[partner]
    strong = (owner == chosen) | (owner == (partner + blocks // 2) % blocks)
    return jnp.where(strong, factor * array, array)


def level_of(rng, dims, cuts, least, top_value):
    gain, own = 1.0, jax.random.fold_in(rng, 6)
    for dim, parts in cuts:
        steps = jnp.exp(jax.random.uniform(jax.random.fold_in(own, dim), (parts,), jnp.float32, least / len(cuts), top_value / len(cuts)))
        gain = gain * jnp.repeat(steps, dims[dim] // parts).reshape([-1 if axis == dim else 1 for axis in range(len(dims))])
    return gain


def split_up(amount, total, most, skew):
    weights = [(1 << 20) // math.isqrt(standing ** skew) + 1 for standing in range(2, amount + 1)]
    spare, holding = total - most - (amount - 1), [1] * (amount - 1)
    while spare > 0:
        candidates = [i for i in range(amount - 1) if holding[i] < most]
        whole, left = sum([weights[i] for i in candidates]), spare
        for i in candidates:
            addition = min(most - holding[i], max(1, left * weights[i] // whole), spare)
            holding[i] = holding[i] + addition
            spare = spare - addition
    return np.array([most] + holding)


def ragged_sizes(key, amount, total, reach, skew):
    if amount == 2:
        one = jax.random.randint(key, (), max(1, total - reach), min(reach, total - 1) + 1)
        return jnp.stack([one, total - one])
    lengths = jnp.asarray(split_up(amount, total, reach, skew), jnp.int32)
    twos = (amount - 1) // 2
    source_of, sink = lengths[1:1 + 2 * twos:2], lengths[2:2 + 2 * twos:2]
    slack = jnp.minimum(source_of - 1, reach - sink)
    moved = jax.random.randint(jax.random.fold_in(key, 1), (twos,), 0, 1 << 20) % (slack + 1)
    lengths = lengths.at[1:1 + 2 * twos:2].set(source_of - moved).at[2:2 + 2 * twos:2].set(sink + moved)
    return lengths[jax.random.permutation(jax.random.fold_in(key, 2), amount)]


def centred(stream_key, extent, spread, bound, cuts=(), kind=jnp.bfloat16):
    factor_of = level_of(stream_key, extent, cuts, -0.22, 0.18) if cuts else 1.0
    entries = jax.random.normal(stream_key, extent, jnp.float32) * spread * factor_of
    return jnp.minimum(jnp.maximum(entries, -bound), bound).astype(kind)


def gaussian_with(key, extent, width, reach, pieces, heavy, kind=jnp.bfloat16):
    result = width * jax.random.normal(key, extent, jnp.float32)
    if pieces:
        result = result * level_of(key, extent, pieces, -0.22, 0.18)
    return jnp.clip(spiked(result, jax.random.fold_in(key, 3), *heavy), -reach, reach).astype(kind)


def setup_inputs(seed: int = 0) -> dict:
    keys = jax.random.split(jax.random.key(seed), 13)
    return {
        "tokens": centred(keys[0], (SEQS, SEQ, D), 1.0, 6.0, ((0, 8), (1, 16))),
        "block_lengths": jax.vmap(lambda own: ragged_sizes(own, BLOCKS, SEQ, BLOCK_MOST, 1))(jax.random.split(keys[1], SEQS)).reshape((SEQS, BLOCKS)).astype(jnp.int32),
        "attn_gain": jnp.clip(1.0 + 0.18 * jax.random.normal(keys[2], (D,), jnp.float32), 0.1, 1.9),
        "query_weight": centred(keys[3], (D, D), D ** -0.5, 0.125, ((0, 16), (1, 8))),
        "key_weight": centred(keys[4], (D, D), D ** -0.5, 0.125, ((0, 16), (1, 8))),
        "value_weight": centred(keys[5], (D, D), D ** -0.5, 0.125, ((0, 16), (1, 8))),
        "out_weight": centred(keys[6], (D, D), (max(D // 256, 2)) ** -0.5, 2.0, ((0, 8), (1, 16))),
        "mlp_gain": jnp.clip(1.0 + 0.18 * jax.random.normal(keys[7], (D,), jnp.float32), 0.1, 1.9),
        "gate_weight": centred(keys[8], (D, FF), D ** -0.5, 0.125, ((0, 16), (1, 8))),
        "up_weight": centred(keys[9], (D, FF), D ** -0.5, 0.125, ((0, 16), (1, 8))),
        "down_weight": centred(keys[10], (FF, D), FF ** -0.5, 0.078125, ((0, 8), (1, 16))),
        "output_grad": gaussian_with(keys[11], (SEQS, SEQ, D), 1.0, 6.0, ((0, 8), (1, 16)), (1, 2, 16, 2.0)),
    }


@jax.custom_vjp
def low(v):
    return lax.optimization_barrier(v.astype(jnp.bfloat16)).astype(jnp.float32)

@jax.custom_vjp
def low_back(v):
    return v

def low_keep(v):
    return (low(v), None)

def low_pass(kept, grad):
    return (grad,)

def back_keep(v):
    return (v, None)

def back_low(kept, grad):
    return (low(grad),)
low.defvjp(low_keep, low_pass)
low_back.defvjp(back_keep, back_low)
norm_eps = 1e-05
masked_score = -1e+30
highest = lax.Precision.HIGHEST

def inverse_rms(values):
    return lax.rsqrt(lax.optimization_barrier(jnp.mean(values * values, axis=-1, keepdims=True)) + norm_eps)

def rotary_tables(row_count, first_row, columns, head_width):
    places = (first_row + jnp.arange(row_count, dtype=jnp.int32)).astype(jnp.float32)
    half_width = head_width // 2
    within = jnp.arange(columns, dtype=jnp.int32) % head_width % half_width
    inverse_freq = 10000.0 ** (within.astype(jnp.float32) * (-2.0 / head_width))
    angles = places[:, None] * inverse_freq[None, :]
    return (jnp.cos(angles), jnp.sin(angles))

def turn_half(values, head_width):
    full_shape = values.shape
    halves = values.reshape(full_shape[:-1] + (full_shape[-1] // head_width, 2, head_width // 2))
    turned = jnp.stack((-halves[..., 1, :], halves[..., 0, :]), axis=-2)
    return turned.reshape(full_shape)

def rotate_forward(values, cosine_table, sine_table, head_width):
    return values * cosine_table + turn_half(values, head_width) * sine_table

def attend_sequence(inputs):
    query_rows, key_rows, values, blocks = inputs
    split_shape = (SEQ, HEADS, HEAD_DIM)
    scores = jnp.einsum('qhd,khd->hqk', query_rows.reshape(split_shape), key_rows.reshape(split_shape), precision=highest) * HEAD_DIM ** (-0.5)
    scores = low_back(scores)
    visible = blocks[None, :] <= blocks[:, None]
    scores = jnp.where(visible[None], scores, masked_score)
    weights = low(jax.nn.softmax(scores, axis=-1))
    attended = jnp.einsum('hqk,khd->qhd', weights, values.reshape(split_shape), precision=highest)
    return attended.reshape(SEQ, D)

def layer(token_float, first_gain, query_matrix, key_matrix, value_matrix, out_matrix, second_gain, gate_matrix, up_matrix, down_matrix, blocks, cosine_table, sine_table):
    flat_tokens = token_float.reshape(SEQS * SEQ, D)
    normed = low(flat_tokens * inverse_rms(flat_tokens) * first_gain)

    def rotated(matrix):
        projected = low_back(jnp.dot(normed, matrix, precision=highest)).reshape(SEQS, SEQ, D)
        return low(rotate_forward(projected, cosine_table, sine_table, HEAD_DIM))
    query_rows = rotated(query_matrix)
    key_rows = rotated(key_matrix)
    value_rows = low(low_back(jnp.dot(normed, value_matrix, precision=highest))).reshape(SEQS, SEQ, D)
    attended = lax.map(jax.checkpoint(attend_sequence), (query_rows, key_rows, value_rows, blocks))
    attended = low(low_back(attended.reshape(SEQS * SEQ, D)))
    residual = flat_tokens + low_back(jnp.dot(attended, out_matrix, precision=highest))
    second = low(residual * inverse_rms(residual) * second_gain)
    gate_preactivation = low_back(jnp.dot(second, gate_matrix, precision=highest))
    upward = low_back(jnp.dot(second, up_matrix, precision=highest))
    hidden_rows = low(jax.nn.silu(gate_preactivation) * upward)
    output = residual + low_back(jnp.dot(hidden_rows, down_matrix, precision=highest))
    return output.reshape(SEQS, SEQ, D)

def reference(tokens, block_lengths, attn_gain, query_weight, key_weight, value_weight, out_weight, mlp_gain, gate_weight, up_weight, down_weight, output_grad):
    block_ends = jnp.cumsum(block_lengths, axis=1).astype(jnp.int32)
    places = jnp.arange(SEQ, dtype=jnp.int32)
    blocks = lax.optimization_barrier(jnp.sum((block_ends[:, None, :] <= places[None, :, None]).astype(jnp.int32), axis=2)).astype(jnp.int32)
    cosine_table, sine_table = rotary_tables(SEQ, 0, D, HEAD_DIM)

    def forward(token_float, first_gain, query_matrix, key_matrix, value_matrix, out_matrix, second_gain, gate_matrix, up_matrix, down_matrix):
        return layer(token_float, first_gain, query_matrix, key_matrix, value_matrix, out_matrix, second_gain, gate_matrix, up_matrix, down_matrix, blocks, cosine_table, sine_table)
    output, pullback = jax.vjp(forward, tokens.astype(jnp.float32), attn_gain, query_weight.astype(jnp.float32), key_weight.astype(jnp.float32), value_weight.astype(jnp.float32), out_weight.astype(jnp.float32), mlp_gain, gate_weight.astype(jnp.float32), up_weight.astype(jnp.float32), down_weight.astype(jnp.float32))
    gradients = pullback(output_grad.astype(jnp.float32))
    return (output.astype(jnp.bfloat16), gradients[0], gradients[1], gradients[2], gradients[3], gradients[4], gradients[5], gradients[6], gradients[7], gradients[8], gradients[9])
```

```python
import functools

import jax
import jax.numpy as jnp
from jax import lax
from jax.experimental import pallas as pl
from jax.experimental.pallas import tpu as pltpu
from jax.sharding import Mesh
from jax.sharding import PartitionSpec as P

HEAD_DIM = 128
SEQ = 2048
TILE = 256
norm_eps = 1e-05
masked_score = -1e30
score_scale = HEAD_DIM ** (-0.5)
log2_e = 1.4426950408889634
f32 = jnp.float32
bf16 = jnp.bfloat16
VMEM_LIMIT = 56 * 1024 * 1024

Y_STEP = {1: 2, 2: 1, 3: 3}


def swap(value, axis, step):
    if axis == "y":
        names, count, step = ("yl", "yh"), 4, Y_STEP[step]
    else:
        names, count = axis, lax.axis_size(axis)
    return lax.ppermute(value, names, [(i, i ^ step) for i in range(count)])


def middle(rows):
    return (rows // 2 + 15) // 16 * 16


def gather4(value, axis):
    half = middle(value.shape[0])
    near1 = swap(value, axis, 1)
    near3 = swap(value, axis, 3)
    far = jnp.concatenate([swap(near3[:half], axis, 1), swap(near1[half:], axis, 3)], axis=0)
    return [value, near1, far, near3]


def scatter4(parts, axis):
    own, part1, part2, part3 = parts
    half = middle(own.shape[0])
    from1 = swap(part2[:half], axis, 1)
    from3 = swap(part2[half:], axis, 3)
    part3 = jnp.concatenate(
        [(part3[:half].astype(f32) + from1.astype(f32)).astype(bf16), part3[half:]], axis=0
    )
    part1 = jnp.concatenate(
        [part1[:half], (part1[half:].astype(f32) + from3.astype(f32)).astype(bf16)], axis=0
    )
    got1, got3 = swap(part1, axis, 1), swap(part3, axis, 3)
    return own.astype(f32) + got1.astype(f32) + got3.astype(f32)


def total4(value, axis):
    return (value + swap(value, axis, 1)) + (swap(value, axis, 2) + swap(value, axis, 3))


def vmem_spec():
    return pl.BlockSpec(memory_space=pltpu.VMEM)


def smem_spec():
    return pl.BlockSpec(memory_space=pltpu.SMEM)


def params():
    return pltpu.CompilerParams(vmem_limit_bytes=VMEM_LIMIT)


def block_at(place_ref, index):
    return pl.ds(pl.multiple_of(place_ref[index] * 128, 128), 128)


def prepare_kernel(place_ref, tok_ref, dy_ref, gain_ref, h1_ref, tok_out, dy_out):
    total = jnp.zeros((128, 128), f32)
    for r in range(16):
        part = tok_ref[:, r * 128 : (r + 1) * 128].astype(f32)
        total = total + part * part
    inverse = lax.rsqrt(jnp.sum(total, axis=1, keepdims=True) / 2048.0 + norm_eps)
    for r in range(16):
        here = slice(r * 128, (r + 1) * 128)
        there = block_at(place_ref, r)
        part = tok_ref[:, there]
        tok_out[:, here] = part
        dy_out[:, here] = dy_ref[:, there]
        h1_ref[:, here] = (part.astype(f32) * inverse * gain_ref[:, here]).astype(bf16)


def prepare(place, tok, dy, gain):
    out = jax.ShapeDtypeStruct((128, 2048), bf16)
    return pl.pallas_call(
        prepare_kernel,
        out_shape=(out, out, out),
        in_specs=[smem_spec(), vmem_spec(), vmem_spec(), vmem_spec()],
        out_specs=(vmem_spec(),) * 3,
        compiler_params=params(),
        name="prepare",
    )(place, tok, dy, gain)


def restore_kernel(place_ref, in_ref, out_ref):
    for r in range(16):
        out_ref[:, block_at(place_ref, r)] = in_ref[:, r * 128 : (r + 1) * 128]


def restore(place, value):
    return pl.pallas_call(
        restore_kernel,
        out_shape=jax.ShapeDtypeStruct(value.shape, value.dtype),
        in_specs=[smem_spec(), vmem_spec()],
        out_specs=vmem_spec(),
        compiler_params=params(),
        name="restore",
    )(place, value)


def dot_nt(left, right):
    return lax.dot_general(left, right, (((1,), (1,)), ((), ())), preferred_element_type=f32)


def dot_nn(left, right):
    return lax.dot_general(left, right, (((1,), (0,)), ((), ())), preferred_element_type=f32)


def dot_tn(left, right):
    return lax.dot_general(left, right, (((0,), (0,)), ((), ())), preferred_element_type=f32)


def qkv_kernel(a0, a1, a2, a3, mine_ref, theirs_ref, cos_ref, sin_ref, out_ref, rows_ref):
    step = pl.program_id(0) * 3 + pl.program_id(1)
    kind = pl.program_id(1)

    @pl.when(step == 0)
    def _():
        for j, ref in enumerate((a0, a1, a2, a3)):
            rows_ref[j * 128 : (j + 1) * 128, :] = ref[...]

    pre = dot_nt(rows_ref[:, :1024], mine_ref[0]) + dot_nt(rows_ref[:, 1024:], theirs_ref[0])

    def store(turned):
        for j in range(4):
            for h in range(2):
                tile = pre[j * 128 : (j + 1) * 128, h * 128 : (h + 1) * 128]
                if turned:
                    tile = tile * cos_ref[...] + pltpu.roll(tile, 64, 1) * sin_ref[...]
                out_ref[j, 0, h, 0] = tile.astype(bf16)

    @pl.when(kind < 2)
    def _():
        store(True)

    @pl.when(kind == 2)
    def _():
        store(False)


def project_qkv(rows, mine, theirs, cosine, sine):
    whole = pl.BlockSpec((128, 2048), lambda s, t: (0, 0))
    weight = pl.BlockSpec((1, 256, 1024), lambda s, t: (s, t, 0))
    table = pl.BlockSpec((128, 128), lambda s, t: (0, 0))
    return pl.pallas_call(
        qkv_kernel,
        grid=(2, 3),
        out_shape=jax.ShapeDtypeStruct((4, 2, 2, 3, 128, 128), bf16),
        in_specs=[whole] * 4 + [weight] * 2 + [table] * 2,
        out_specs=pl.BlockSpec((4, 1, 2, 1, 128, 128), lambda s, t: (0, s, 0, t, 0, 0)),
        scratch_shapes=[pltpu.VMEM((512, 2048), bf16)],
        compiler_params=params(),
        cost_estimate=pl.CostEstimate(
            flops=2 * 512 * 2048 * 1536, bytes_accessed=10 << 20, transcendentals=0
        ),
        name="project_qkv",
    )(*rows, mine, theirs, cosine, sine)


def visible_end(ends_ref, first):
    places = first + lax.broadcasted_iota(jnp.int32, (1, TILE), 1)
    end = jnp.full((1, TILE), SEQ, jnp.int32)
    for j in range(10, -1, -1):
        end = jnp.where(places < ends_ref[j], ends_ref[j], end)
    return end


def key_blocks(i):
    return min(i + 2, SEQ // TILE)


def rows_of(ref, kind, i):
    return ref[2 * i : 2 * i + 2, kind].reshape(TILE, HEAD_DIM)


def masked(scores, end, kb):
    places = kb * TILE + lax.broadcasted_iota(jnp.int32, (TILE, TILE), 0)
    return jnp.where(places < end, scores, masked_score)


def attend_kernel(ends_ref, qkv_ref, low_ref, out_ref, lse_ref, score_ref, value_ref):
    for i in range(SEQ // TILE):
        value_ref[:, i * TILE : (i + 1) * TILE] = rows_of(qkv_ref, 2, i).astype(f32).T.astype(bf16)
    for i in range(SEQ // TILE):
        query = rows_of(qkv_ref, 0, i)
        end = visible_end(ends_ref, i * TILE)
        top = jnp.full((8, TILE), masked_score, f32)
        for kb in range(key_blocks(i)):
            scores = dot_nt(rows_of(qkv_ref, 1, kb), query) * (score_scale * log2_e)
            if kb >= i:
                scores = masked(scores, end, kb)
            score_ref[kb * TILE : (kb + 1) * TILE, :] = scores
            top = jnp.maximum(top, jnp.max(scores.reshape(TILE // 8, 8, TILE), axis=0))
        top = jnp.max(top, axis=0, keepdims=True)
        total = jnp.zeros((8, TILE), f32)
        acc = jnp.zeros((HEAD_DIM, TILE), f32)
        for kb in range(key_blocks(i)):
            weights = jnp.exp2(score_ref[kb * TILE : (kb + 1) * TILE, :] - top)
            total = total + jnp.sum(weights.reshape(TILE // 8, 8, TILE), axis=0)
            acc = acc + dot_nn(value_ref[:, kb * TILE : (kb + 1) * TILE], weights.astype(bf16))
        total = jnp.sum(total, axis=0, keepdims=True)
        attended = (acc / total).T
        out_ref[i * TILE : (i + 1) * TILE, :] = attended
        low_ref[2 * i : 2 * i + 2] = attended.astype(bf16).reshape(2, 128, HEAD_DIM)
        lse_ref[:, i * TILE : (i + 1) * TILE] = top + jnp.log2(total)


def attend(ends, qkv):
    return pl.pallas_call(
        attend_kernel,
        out_shape=(
            jax.ShapeDtypeStruct((16, 128, HEAD_DIM), bf16),
            jax.ShapeDtypeStruct((SEQ, HEAD_DIM), f32),
            jax.ShapeDtypeStruct((1, SEQ), f32),
        ),
        in_specs=[smem_spec(), vmem_spec()],
        out_specs=(vmem_spec(),) * 3,
        scratch_shapes=[pltpu.VMEM((SEQ, TILE), f32), pltpu.VMEM((HEAD_DIM, SEQ), bf16)],
        compiler_params=params(),
        cost_estimate=pl.CostEstimate(
            flops=4 * 2048 * 2048 * 128, bytes_accessed=4 << 20, transcendentals=2 << 20
        ),
        name="attend",
    )(ends, qkv)


def attend_back_kernel(
    ends_ref, qkv_ref, grad_ref, out_ref, lse_ref, cos_ref, sin_ref, dqkv_ref, dk_ref, dv_ref
):
    dk_ref[...] = jnp.zeros_like(dk_ref)
    dv_ref[...] = jnp.zeros_like(dv_ref)

    def turn_back(gradient, i):
        here = slice(i * TILE, (i + 1) * TILE)
        gradient = gradient * score_scale
        turned = gradient * cos_ref[here, :] - pltpu.roll(gradient, 64, 1) * sin_ref[here, :]
        return turned.astype(bf16).reshape(2, 128, HEAD_DIM)

    for i in range(SEQ // TILE):
        here = slice(i * TILE, (i + 1) * TILE)
        query = rows_of(qkv_ref, 0, i)
        grad = grad_ref[2 * i : 2 * i + 2].reshape(TILE, HEAD_DIM)
        product = jnp.sum(grad.astype(f32) * out_ref[here, :], axis=1, keepdims=True)
        delta = jnp.broadcast_to(product, (TILE, 128)).T[0:1, :]
        lse = lse_ref[:, here]
        end = visible_end(ends_ref, i * TILE)
        dq = jnp.zeros((TILE, HEAD_DIM), f32)
        for kb in range(key_blocks(i)):
            there = slice(kb * TILE, (kb + 1) * TILE)
            key = rows_of(qkv_ref, 1, kb)
            scores = dot_nt(key, query) * (score_scale * log2_e)
            if kb >= i:
                scores = masked(scores, end, kb)
            probs = jnp.exp2(scores - lse)
            dv_ref[there, :] += dot_nn(probs.astype(bf16), grad)
            dprobs = dot_nt(rows_of(qkv_ref, 2, kb), grad)
            dscores = (probs * (dprobs - delta)).astype(bf16)
            dk_ref[there, :] += dot_nn(dscores, query)
            dq = dq + dot_tn(dscores, key)
        dqkv_ref[2 * i : 2 * i + 2, 0] = turn_back(dq, i)
    for i in range(SEQ // TILE):
        here = slice(i * TILE, (i + 1) * TILE)
        dqkv_ref[2 * i : 2 * i + 2, 1] = turn_back(dk_ref[here, :], i)
        dqkv_ref[2 * i : 2 * i + 2, 2] = dv_ref[here, :].astype(bf16).reshape(2, 128, HEAD_DIM)


def attend_back(ends, qkv, grad, out, lse, cosine, sine):
    return pl.pallas_call(
        attend_back_kernel,
        out_shape=jax.ShapeDtypeStruct((16, 3, 128, HEAD_DIM), bf16),
        in_specs=[smem_spec()] + [vmem_spec()] * 6,
        out_specs=vmem_spec(),
        scratch_shapes=[pltpu.VMEM((SEQ, HEAD_DIM), f32), pltpu.VMEM((SEQ, HEAD_DIM), f32)],
        compiler_params=params(),
        cost_estimate=pl.CostEstimate(
            flops=10 * 2048 * 2048 * 128, bytes_accessed=8 << 20, transcendentals=2 << 20
        ),
        name="attend_back",
    )(ends, qkv, grad, out, lse, cosine, sine)


def gather_weight(shard):
    along_z = jnp.concatenate(gather4(shard, "z"), axis=1)
    own, near1, far, near3 = gather4(along_z, "y")
    mine = jnp.stack(
        [jnp.concatenate([own, far], axis=1), jnp.concatenate([near1, near3], axis=1)], axis=0
    )
    return mine, swap(mine, "c", 1)


def scatter_weight(grad):
    got = swap(grad[:, :, 1024:], "c", 1)
    mine = (grad[:, :, :1024].astype(f32) + got.astype(f32)).astype(bf16)
    along_y = scatter4(
        [mine[0, :, :512], mine[1, :, :512], mine[0, :, 512:], mine[1, :, 512:]], "y"
    ).astype(bf16)
    return scatter4([along_y[:, b * 128 : (b + 1) * 128] for b in range(4)], "z")


def rotary(count):
    places = jnp.arange(count, dtype=jnp.int32).astype(f32)
    within = jnp.arange(HEAD_DIM, dtype=jnp.int32) % (HEAD_DIM // 2)
    inverse_freq = 10000.0 ** (within.astype(f32) * (-2.0 / HEAD_DIM))
    angles = places[:, None] * inverse_freq[None, :]
    sign = jnp.where(jnp.arange(HEAD_DIM) < HEAD_DIM // 2, -1.0, 1.0).astype(f32)
    return jnp.cos(angles), jnp.sin(angles) * sign


def inverse_rms(values):
    return lax.rsqrt(jnp.mean(values * values, axis=-1, keepdims=True) + norm_eps)


def norm_back(grad_normed, values, inverse, gain):
    scaled = grad_normed * gain
    gain_part = jnp.sum(grad_normed * values * inverse, axis=0)
    inner = jnp.mean(scaled * values, axis=-1, keepdims=True)
    return inverse * scaled - values * inverse**3 * inner, gain_part


def on_device(
    tokens,
    block_lengths,
    attn_gain,
    query_weight,
    key_weight,
    value_weight,
    out_weight,
    mlp_gain,
    gate_weight,
    up_weight,
    down_weight,
    output_grad,
):
    x, yl, yh, z, c = (lax.axis_index(name) for name in ("x", "yl", "yh", "z", "c"))
    blk = (yh * 4 + z) * 2 + c
    rel = jnp.arange(16, dtype=jnp.int32)
    place = ((yh ^ ((rel >> 2) & 1)) * 4 + (z ^ (rel & 3))) * 2 + (c ^ (rel >> 3))
    chosen = place[:, None] == rel[None, :]

    def relative(gain):
        return jnp.sum(jnp.where(chosen[:, :, None], gain.reshape(1, 16, 128), 0.0), axis=1)

    def absolute(gain):
        return jnp.sum(jnp.where(chosen[:, :, None], gain.reshape(16, 1, 128), 0.0), axis=0)

    first_gain = relative(attn_gain).reshape(1, 2048)
    second_gain = relative(mlp_gain).reshape(1, 2048)
    cosine, sine = rotary(SEQ)
    own_cosine = lax.dynamic_slice_in_dim(cosine, blk * 128, 128, 0)
    own_sine = lax.dynamic_slice_in_dim(sine, blk * 128, 128, 0)
    sequence = (x ^ (blk >> 2)) * 2 + yl
    ends = jnp.cumsum(lax.dynamic_slice_in_dim(block_lengths, sequence, 1, 0)[0])

    normed1, tok, dy = prepare(place, tokens[0], output_grad[0], first_gain)
    tok = tok.astype(f32)
    rows1 = gather4(normed1, "x")
    shard1 = jnp.concatenate([query_weight.T, key_weight.T, value_weight.T], axis=0)
    mine1, theirs1 = gather_weight(shard1)
    shard2 = jnp.concatenate([out_weight, gate_weight.T, up_weight.T, down_weight], axis=0)
    mine2, theirs2 = gather_weight(shard2)
    weight1 = jnp.concatenate([mine1, theirs1], axis=2)
    weight2 = jnp.concatenate([mine2, theirs2], axis=2)
    w_out, w_gate, w_up, w_down = (
        weight2[:, :256],
        weight2[:, 256:944],
        weight2[:, 944:1632],
        weight2[:, 1632:],
    )

    blkaxes = ("yh", "z", "c")
    qkv_own = project_qkv(rows1, mine1, theirs1, own_cosine, own_sine)
    qkv = lax.all_to_all(
        qkv_own.reshape(16, 3, 128, 128), blkaxes, split_axis=0, concat_axis=0, tiled=True
    )
    low, attended, lse = attend(ends, qkv)
    low = lax.all_to_all(low, blkaxes, split_axis=0, concat_axis=0, tiled=True)
    low = low.reshape(4, 2, 2, 128, 128)
    part = jnp.einsum(
        "jshrk,shkd->jrd", low, w_out.reshape(2, 2, 128, 2048), preferred_element_type=f32
    ).astype(bf16)
    residual = tok + scatter4(list(part), "x")
    inverse2 = inverse_rms(residual)
    normed2 = (residual * inverse2 * second_gain).astype(bf16)

    dy_rows = jnp.concatenate(gather4(dy, "x"), axis=0)
    rows2 = jnp.concatenate(gather4(normed2, "x"), axis=0)
    gate = jnp.einsum("md,srd->smr", rows2, w_gate, preferred_element_type=f32)
    up = jnp.einsum("md,srd->smr", rows2, w_up, preferred_element_type=f32)
    sigmoid = jax.nn.sigmoid(gate)
    silu = gate * sigmoid
    hidden = (silu * up).astype(bf16)
    d_hidden = jnp.einsum("md,srd->smr", dy_rows, w_down, preferred_element_type=f32)
    d_gate = (d_hidden * up * sigmoid * (1.0 + gate * (1.0 - sigmoid))).astype(bf16)
    d_up = (d_hidden * silu).astype(bf16)
    part = (
        jnp.einsum("smr,srd->md", d_gate, w_gate, preferred_element_type=f32)
        + jnp.einsum("smr,srd->md", d_up, w_up, preferred_element_type=f32)
    ).astype(bf16)
    d_normed2 = scatter4(list(part.reshape(4, 128, 2048)), "x")
    back2, second_part = norm_back(d_normed2, residual, inverse2, second_gain)
    d_residual = dy.astype(f32) + back2
    d_attn = d_residual.astype(bf16)
    rows3 = jnp.concatenate(gather4(d_attn, "x"), axis=0)

    part = jnp.einsum("smr,srd->md", hidden, w_down, preferred_element_type=f32).astype(bf16)
    output = (residual + scatter4(list(part.reshape(4, 128, 2048)), "x")).astype(bf16)
    layer_output = restore(place, output)[None]

    d_out = jnp.einsum(
        "jrd,shkd->jshrk",
        rows3.reshape(4, 128, 2048),
        w_out.reshape(2, 2, 128, 2048),
        preferred_element_type=f32,
    ).astype(bf16)
    d_out = lax.all_to_all(
        d_out.reshape(16, 128, 128), blkaxes, split_axis=0, concat_axis=0, tiled=True
    )
    dqkv = attend_back(ends, qkv, d_out, attended, lse, cosine, sine)

    grad_gate = jnp.einsum("smr,md->srd", d_gate, rows2, preferred_element_type=f32).astype(bf16)
    grad_up = jnp.einsum("smr,md->srd", d_up, rows2, preferred_element_type=f32).astype(bf16)
    grad_down = jnp.einsum("smr,md->srd", hidden, dy_rows, preferred_element_type=f32).astype(bf16)
    grad_out = (
        jnp.einsum(
            "jshrk,jrd->shkd", low, rows3.reshape(4, 128, 2048), preferred_element_type=f32
        )
        .astype(bf16)
        .reshape(2, 256, 2048)
    )
    grads2 = scatter_weight(jnp.concatenate([grad_out, grad_gate, grad_up, grad_down], axis=1))

    dqkv = lax.all_to_all(dqkv, blkaxes, split_axis=0, concat_axis=0, tiled=True)
    dqkv = dqkv.reshape(4, 2, 2, 3, 128, 128)
    part = jnp.einsum(
        "jshtrk,sthkd->jrd",
        dqkv,
        weight1.reshape(2, 3, 2, 128, 2048),
        preferred_element_type=f32,
    ).astype(bf16)
    d_normed1 = scatter4(list(part), "x")
    rows1_all = jnp.stack(rows1, axis=0)
    grad1 = (
        jnp.einsum("jshtrk,jrd->sthkd", dqkv, rows1_all, preferred_element_type=f32)
        .astype(bf16)
        .reshape(2, 768, 2048)
    )
    grads1 = scatter_weight(grad1)
    back1, first_part = norm_back(d_normed1, tok, inverse_rms(tok), first_gain)
    input_grad = restore(place, d_residual + back1)[None]

    gains = jnp.concatenate([absolute(first_part), absolute(second_part)], axis=0)
    for axis in ("x", "y", "z"):
        gains = total4(gains, axis)
    gains = gains + swap(gains, "c", 1)
    return (
        layer_output,
        input_grad,
        gains[:16].reshape(2048),
        grads1[:256].T,
        grads1[256:512].T,
        grads1[512:].T,
        grads2[:256],
        gains[16:].reshape(2048),
        grads2[256:944].T,
        grads2[944:1632].T,
        grads2[1632:],
    )


def solution(mesh):
    fine = Mesh(mesh.devices.reshape(4, 2, 2, 4, 2), ("x", "yl", "yh", "z", "c"))
    head, blk = ("x", "yl"), ("yh", "z", "c")
    rows = P(head, blk, None)
    wide, tall = P(blk, head), P(head, blk)
    return jax.shard_map(
        on_device,
        mesh=fine,
        in_specs=(rows, P(), P(), wide, wide, wide, tall, P(), wide, wide, tall, rows),
        out_specs=(rows, rows, P(), wide, wide, wide, tall, P(), wide, wide, tall),
        check_vma=False,
    )
```

```python
import functools

import jax
import jax.numpy as jnp
from jax import lax
from jax.experimental import pallas as pl
from jax.experimental.pallas import tpu as pltpu
from jax.sharding import Mesh
from jax.sharding import PartitionSpec as P

HEAD_DIM = 128
SEQ = 2048
TILE = 256
norm_eps = 1e-05
masked_score = -1e30
score_scale = HEAD_DIM ** (-0.5)
log2_e = 1.4426950408889634
f32 = jnp.float32
bf16 = jnp.bfloat16
VMEM_LIMIT = 56 * 1024 * 1024

Y_STEP = {1: 2, 2: 1, 3: 3}


def swap(value, axis, step):
    if axis == "y":
        names, count, step = ("yl", "yh"), 4, Y_STEP[step]
    else:
        names, count = axis, lax.axis_size(axis)
    return lax.ppermute(value, names, [(i, i ^ step) for i in range(count)])


def middle(rows):
    return (rows // 2 + 15) // 16 * 16


def gather4(value, axis, hold=()):
    near = swap(value, axis, 1), swap(value, axis, 3)
    return gather_far(value, near, axis, hold)


def gather_far(value, near, axis, hold=()):
    half = middle(value.shape[0]) if value.ndim == 2 else value.shape[0] // 2
    near1, near3 = near
    far1 = swap(after(near3[:half], *hold), axis, 1)
    return value, near1, far1, swap(near1[half:], axis, 3), near3


def add(*values):
    return functools.reduce(lambda a, b: a + b, [value.astype(f32) for value in values])


def after(value, *earlier):
    return lax.optimization_barrier((value, *earlier))[0] if earlier else value


def far_sums(part2):
    rows = part2[0].shape[0]
    half = middle(rows) if part2[0].ndim == 2 else rows // 2
    return (
        add(*[term[:half] for term in part2]).astype(bf16),
        add(*[term[half:] for term in part2]).astype(bf16),
    )


def scatter_far(part2, axis):
    far_a, far_b = far_sums(part2)
    return swap(far_a, axis, 1), swap(far_b, axis, 3)


def near_sums(part1, part3, far):
    from1, from3 = far
    half = from1.shape[0]
    part1 = jnp.concatenate(
        [
            add(*[term[:half] for term in part1]).astype(bf16),
            add(from3, *[term[half:] for term in part1]).astype(bf16),
        ],
        axis=0,
    )
    part3 = jnp.concatenate(
        [
            add(from1, *[term[:half] for term in part3]).astype(bf16),
            add(*[term[half:] for term in part3]).astype(bf16),
        ],
        axis=0,
    )
    return part1, part3


def scatter_near(part1, part3, far, axis, hold=()):
    part1, part3 = near_sums(part1, part3, far)
    return swap(after(part1, *hold), axis, 1), swap(part3, axis, 3)


def scatter4(parts, axis):
    own, part1, part2, part3 = parts
    return add(*scatter_near(part1, part3, scatter_far(part2, axis), axis), *own)


def pairs(mine, got):
    return [[mine[k], got[k]] for k in range(4)]


def total4(value, axis):
    return (value + swap(value, axis, 1)) + (swap(value, axis, 2) + swap(value, axis, 3))


def vmem_spec():
    return pl.BlockSpec(memory_space=pltpu.VMEM)


def smem_spec():
    return pl.BlockSpec(memory_space=pltpu.SMEM)


def params():
    return pltpu.CompilerParams(vmem_limit_bytes=VMEM_LIMIT)


def block_at(place_ref, index):
    return pl.ds(pl.multiple_of(place_ref[index] * 128, 128), 128)


def prepare_kernel(place_ref, tok_ref, dy_ref, gain_ref, h1_ref, tok_out, dy_out):
    total = jnp.zeros((128, 128), f32)
    for r in range(16):
        part = tok_ref[:, r * 128 : (r + 1) * 128].astype(f32)
        total = total + part * part
    inverse = lax.rsqrt(jnp.sum(total, axis=1, keepdims=True) / 2048.0 + norm_eps)
    for r in range(16):
        here = slice(r * 128, (r + 1) * 128)
        there = block_at(place_ref, r)
        part = tok_ref[:, there]
        tok_out[:, here] = part
        dy_out[:, here] = dy_ref[:, there]
        h1_ref[:, here] = (part.astype(f32) * inverse * gain_ref[:, here]).astype(bf16)


def prepare(place, tok, dy, gain):
    out = jax.ShapeDtypeStruct((128, 2048), bf16)
    return pl.pallas_call(
        prepare_kernel,
        out_shape=(out, out, out),
        in_specs=[smem_spec(), vmem_spec(), vmem_spec(), vmem_spec()],
        out_specs=(vmem_spec(),) * 3,
        compiler_params=params(),
        cost_estimate=cost(2.5),
        name="prepare",
    )(place, tok, dy, gain)


def restore_kernel(place_ref, in_ref, out_ref):
    for r in range(16):
        out_ref[:, block_at(place_ref, r)] = in_ref[:, r * 128 : (r + 1) * 128]


def restore(place, value):
    return pl.pallas_call(
        restore_kernel,
        out_shape=jax.ShapeDtypeStruct(value.shape, value.dtype),
        in_specs=[smem_spec(), vmem_spec()],
        out_specs=vmem_spec(),
        compiler_params=params(),
        cost_estimate=cost(2),
        name="restore",
    )(place, value)


def dot_nt(left, right):
    return lax.dot_general(left, right, (((1,), (1,)), ((), ())), preferred_element_type=f32)


def dot_nn(left, right):
    return lax.dot_general(left, right, (((1,), (0,)), ((), ())), preferred_element_type=f32)


def dot_tn(left, right):
    return lax.dot_general(left, right, (((0,), (0,)), ((), ())), preferred_element_type=f32)


def any_spec():
    return pl.BlockSpec(memory_space=pl.ANY)


def pieces_of(order):
    found = []
    for core in range(2):
        for second in range(4):
            for first in range(4):
                z, y = (first, second) if order == "zy" else (second, first)
                slab, turn = y & 1, y >> 1
                if second == 2:
                    array, entry = (2, first) if first < 2 else (3, first - 2)
                else:
                    array, entry = {0: 0, 1: 1, 3: 4}[second], first
                found.append((core * 5 + array, entry, slab, core * 8 + turn * 4 + z))
    return found


GROUP_A, GROUP_B = 1024, 1040
MLP_ROWS = {
    "gate": ((0, 0, 688, 0),),
    "up": ((0, 688, 336, 0), (1, 0, 352, 336)),
    "down": ((1, 352, 688, 0),),
}


class Loader:
    def __init__(self, sems, source_ref=None):
        self.sems = sems
        self.source_ref = source_ref
        self.used = 0

    def copy(self, source, target):
        made = pltpu.make_async_copy(source, target, self.sems.at[self.used])
        self.used += 1
        made.start()
        return made

    def weight(self, refs, first_row, target, source_ref=None):
        source_ref = self.source_ref if source_ref is None else source_ref
        waits = ([], [])
        rows = target.shape[1]
        for core in range(2):
            for k in range(16):
                slab, block = k >> 3, core * 8 + (k & 7)
                waits[slab].append(
                    self.copy(
                        refs[core].at[source_ref[k], first_row : first_row + rows],
                        target.at[slab, :, block * 128 : (block + 1) * 128],
                    )
                )
        return waits

    def mlp_weight(self, pieces, name, target):
        waits = ([], [])
        for group, first_row, rows, at in MLP_ROWS[name]:
            refs = pieces[group * 10 : group * 10 + 10]
            for array, entry, slab, block in pieces_of(("zy", "yz")[group]):
                waits[slab].append(
                    self.copy(
                        refs[array].at[entry, first_row : first_row + rows],
                        target.at[slab, at : at + rows, block * 128 : (block + 1) * 128],
                    )
                )
        return waits

    def rows(self, refs, target):
        return [
            self.copy(ref, target.at[first : first + ref.shape[0]])
            for ref, first in zip(refs, (0, 128, 256, 320, 384))
        ]


def wait_all(copies):
    for made in copies:
        made.wait()


def cost(micros):
    return pl.CostEstimate(flops=int(micros * 1.15e9), bytes_accessed=0, transcendentals=0)


def kernel_call(kernel, out_shape, args, scratch, copies, micros, name, smem=0):
    specs = [any_spec()] * (len(args) - smem)
    return pl.pallas_call(
        kernel,
        out_shape=out_shape,
        in_specs=[smem_spec()] * smem + specs,
        out_specs=jax.tree.map(lambda _: vmem_spec(), out_shape),
        scratch_shapes=list(scratch) + [pltpu.SemaphoreType.DMA((copies,))],
        compiler_params=params(),
        cost_estimate=cost(micros),
        name=name,
    )(*args)


def shape_of(*dims, dtype=bf16):
    return jax.ShapeDtypeStruct(dims, dtype)


ROWS = pltpu.VMEM((512, 2048), bf16)


def weight_scratch(rows):
    return pltpu.VMEM((2, rows, 2048), bf16)


def stack_kernel(own, near1, far, near3, out_ref, sems):
    load = Loader(sems)
    wait_all([load.copy(ref, out_ref.at[n]) for n, ref in enumerate((own, near1, far, near3))])


def stacked(parts):
    own = parts[0]
    return pl.pallas_call(
        stack_kernel,
        out_shape=shape_of(4, *own.shape),
        in_specs=[any_spec()] * 4,
        out_specs=vmem_spec(),
        scratch_shapes=[pltpu.SemaphoreType.DMA((4,))],
        compiler_params=params(),
        cost_estimate=cost(2.5),
        name="stack",
    )(*parts)


def qkv_kernel(source_ref, *refs):
    rows, weights = refs[:5], refs[5:7]
    cos_ref, sin_ref, out_ref, acts, weight, tables, sems = refs[7:]
    load = Loader(sems, source_ref)
    small = [load.copy(cos_ref, tables.at[0]), load.copy(sin_ref, tables.at[1])]
    acts_in = load.rows(rows, acts)
    arrived = load.weight(weights, 0, weight)
    wait_all(small + acts_in)
    for slab in range(2):
        wait_all(arrived[slab])
        for kind in range(3):
            pre = dot_nt(acts[...], weight[slab, kind * 256 : (kind + 1) * 256])
            for head in range(2):
                for j in range(4):
                    tile = pre[j * 128 : (j + 1) * 128, head * 128 : (head + 1) * 128]
                    if kind < 2:
                        tile = tile * tables[0] + pltpu.roll(tile, 64, 1) * tables[1]
                    out_ref[j * 4 + slab * 2 + head, kind] = tile.astype(bf16)


def project_qkv(source, rows, weights, cosine, sine):
    return kernel_call(
        qkv_kernel,
        shape_of(16, 3, 128, 128),
        (source, *rows, *weights, cosine, sine),
        [ROWS, weight_scratch(768), pltpu.VMEM((2, 128, 128), f32)],
        7 + 32,
        10,
        "project_qkv",
        smem=1,
    )


def out_kernel(source_ref, low_ref, mine_ref, theirs_ref, part_ref, low, acts, weight, sems):
    load = Loader(sems, source_ref)
    low_in = load.copy(low_ref, low)
    arrived = load.weight((mine_ref, theirs_ref), 768, weight)
    low_in.wait()
    for p in range(16):
        j, slab, head = p >> 2, (p >> 1) & 1, p & 1
        acts[slab, j * 128 : (j + 1) * 128, head * 128 : (head + 1) * 128] = low[p]
    wait_all(arrived[0] + arrived[1])
    for j in range(0, 4, 2):
        here = slice(j * 128, (j + 2) * 128)
        part = dot_nn(acts[0, here], weight[0]) + dot_nn(acts[1, here], weight[1])
        part_ref[j : j + 2] = part.astype(bf16).reshape(2, 128, 2048)


def project_out(source, low, weights):
    return kernel_call(
        out_kernel,
        shape_of(4, 128, 2048),
        (source, low, *weights),
        [
            pltpu.VMEM((16, 128, 128), bf16),
            pltpu.VMEM((2, 512, 256), bf16),
            weight_scratch(256),
        ],
        1 + 32,
        5,
        "project_out",
        smem=1,
    )


def mlp_kernel(*refs):
    rows, dy_rows, weights = refs[:5], refs[5:10], refs[10:30]
    hidden_ref, d_gate_ref, d_up_ref, part_ref = refs[30:34]
    acts, acts_dy, w_gate, w_up, w_down, acc, sems = refs[34:]
    load = Loader(sems)
    acts_in = load.rows(rows, acts)
    gates = load.mlp_weight(weights, "gate", w_gate)
    ups = load.mlp_weight(weights, "up", w_up)
    dy_in = load.rows(dy_rows, acts_dy)
    downs = load.mlp_weight(weights, "down", w_down)
    wait_all(acts_in)
    for slab in range(2):
        wait_all(gates[slab])
        gate = dot_nt(acts[...], w_gate[slab])
        wait_all(ups[slab])
        up = dot_nt(acts[...], w_up[slab])
        if slab == 0:
            wait_all(dy_in)
        wait_all(downs[slab])
        d_hidden = dot_nt(acts_dy[...], w_down[slab])
        sigmoid = 1.0 / (1.0 + jnp.exp(-gate))
        silu = gate * sigmoid
        hidden_ref[slab] = (silu * up).astype(bf16)
        d_gate_ref[slab] = (d_hidden * up * sigmoid * (1.0 + gate * (1.0 - sigmoid))).astype(bf16)
        d_up_ref[slab] = (d_hidden * silu).astype(bf16)
        part = dot_nn(d_gate_ref[slab], w_gate[slab]) + dot_nn(d_up_ref[slab], w_up[slab])
        if slab == 0:
            acc[...] = part
        else:
            part_ref[...] = (acc[...] + part).astype(bf16).reshape(4, 128, 2048)


def mlp(rows, dy_rows, weights):
    return kernel_call(
        mlp_kernel,
        (shape_of(2, 512, 688),) * 3 + (shape_of(4, 128, 2048),),
        (*rows, *dy_rows, *weights),
        [ROWS, ROWS]
        + [weight_scratch(688)] * 3
        + [pltpu.VMEM((512, 2048), f32)],
        10 + 128,
        28,
        "mlp",
    )


def down_kernel(hidden_ref, *refs):
    weights, (part_ref, hidden, weight, sems) = refs[:20], refs[20:]
    load = Loader(sems)
    hidden_in = load.copy(hidden_ref, hidden)
    arrived = load.mlp_weight(weights, "down", weight)
    hidden_in.wait()
    wait_all(arrived[0] + arrived[1])
    part = dot_nn(hidden[0], weight[0]) + dot_nn(hidden[1], weight[1])
    part_ref[...] = part.astype(bf16).reshape(4, 128, 2048)


def project_down(hidden, weights):
    return kernel_call(
        down_kernel,
        shape_of(4, 128, 2048),
        (hidden, *weights),
        [pltpu.VMEM((2, 512, 688), bf16), weight_scratch(688)],
        1 + 32,
        8,
        "project_down",
    )


def feature_grads(acts, rows, store):
    for slab in range(2):
        for quarter in range(4):
            value = dot_tn(acts[slab], rows[:, quarter * 512 : (quarter + 1) * 512])
            core, turn = divmod(quarter, 2)
            for z in range(4):
                block = value[:, z * 128 : (z + 1) * 128].astype(bf16)
                store(core, slab * 8 + turn * 4 + z, block)


def mlp_grad_kernel(d_gate_ref, d_up_ref, hidden_ref, *refs):
    rows, dy_rows, outs, (acts, acts_dy, hidden, sems) = (
        refs[:5],
        refs[5:10],
        refs[10:12],
        refs[12:],
    )
    load = Loader(sems)
    acts_in = load.rows(rows, acts)
    hidden_in = [
        load.copy(ref, hidden.at[n]) for n, ref in enumerate((d_gate_ref, d_up_ref, hidden_ref))
    ]
    dy_in = load.rows(dy_rows, acts_dy)
    wait_all(acts_in)
    for n in range(3):
        hidden_in[n].wait()
        if n == 2:
            wait_all(dy_in)

        def store(core, k, block, first=n * 688):
            y = ((k >> 2) & 1) * 2 + (k >> 3)
            outs[core][y, k & 3, first : first + 688] = block

        feature_grads(hidden.at[n], acts if n < 2 else acts_dy, store)


def mlp_grad(d_gate, d_up, hidden, rows, dy_rows):
    return kernel_call(
        mlp_grad_kernel,
        (shape_of(4, 4, 2064, 128),) * 2,
        (d_gate, d_up, hidden, *rows, *dy_rows),
        [ROWS, ROWS, pltpu.VMEM((3, 2, 512, 688), bf16)],
        13,
        18,
        "mlp_grad",
    )


def out_back_kernel(source_ref, *refs):
    rows, weights = refs[:5], refs[5:7]
    out_ref, acts, weight, sems = refs[7:]
    load = Loader(sems, source_ref)
    acts_in = load.rows(rows, acts)
    arrived = load.weight(weights, 768, weight)
    wait_all(acts_in)
    for slab in range(2):
        wait_all(arrived[slab])
        value = dot_nt(acts[...], weight[slab]).astype(bf16)
        for j in range(4):
            for head in range(2):
                out_ref[j * 4 + slab * 2 + head] = value[
                    j * 128 : (j + 1) * 128, head * 128 : (head + 1) * 128
                ]


def out_back(source, rows, weights):
    return kernel_call(
        out_back_kernel,
        shape_of(16, 128, 128),
        (source, *rows, *weights),
        [ROWS, weight_scratch(256)],
        5 + 32,
        6,
        "out_back",
        smem=1,
    )


def unpack_heads(source, target):
    for p in range(16):
        j, slab, head = p >> 2, (p >> 1) & 1, p & 1
        for kind in range(3):
            column = (kind * 2 + head) * 128
            target[slab, j * 128 : (j + 1) * 128, column : column + 128] = source[p, kind]


def qkv_back_kernel(source_ref, dqkv_ref, mine_ref, theirs_ref, *refs):
    rows, (part_ref, gain_ref, dqkv, acts, weight, tokens, acc, sems) = refs[:5], refs[5:]
    load = Loader(sems, source_ref)
    dqkv_in = load.copy(dqkv_ref, dqkv)
    arrived = load.weight((mine_ref, theirs_ref), 0, weight)
    tokens_in = load.rows(rows, tokens)
    dqkv_in.wait()
    unpack_heads(dqkv, acts)
    for slab in range(2):
        wait_all(arrived[slab])
        part = dot_nn(acts[slab], weight[slab])
        if slab == 0:
            acc[...] = part
        else:
            acc[...] += part
            part_ref[...] = acc[...].astype(bf16).reshape(4, 128, 2048)
    wait_all(tokens_in)
    gain_ref[...] = jnp.zeros_like(gain_ref)
    for first in range(0, 512, 64):
        values = tokens[first : first + 64].astype(f32)
        inverse = lax.rsqrt(jnp.sum(values * values, axis=1, keepdims=True) / 2048.0 + norm_eps)
        product = acc[first : first + 64] * values * inverse
        gain_ref[...] += jnp.sum(product.reshape(8, 8, 2048), axis=0)


def qkv_back(source, dqkv, weights, token_rows):
    return kernel_call(
        qkv_back_kernel,
        (shape_of(4, 128, 2048), shape_of(8, 2048, dtype=f32)),
        (source, dqkv, *weights, *token_rows),
        [
            pltpu.VMEM((16, 3, 128, 128), bf16),
            pltpu.VMEM((2, 512, 768), bf16),
            weight_scratch(768),
            ROWS,
            pltpu.VMEM((512, 2048), f32),
        ],
        1 + 32 + 5,
        12,
        "qkv_back",
        smem=1,
    )


def qkv_grad_kernel(dqkv_ref, low_ref, *refs):
    rows1, rows3, outs = refs[:5], refs[5:10], refs[10:12]
    dqkv, low, acts, low_acts, in1, in3, sems = refs[12:]
    load = Loader(sems)
    low_in = load.copy(low_ref, low)
    in3_in = load.rows(rows3, in3)
    dqkv_in = load.copy(dqkv_ref, dqkv)
    in1_in = load.rows(rows1, in1)
    low_in.wait()
    for p in range(16):
        j, slab, head = p >> 2, (p >> 1) & 1, p & 1
        low_acts[slab, j * 128 : (j + 1) * 128, head * 128 : (head + 1) * 128] = low[p]
    wait_all(in3_in)

    def store_at(first):
        def store(core, k, block):
            y = ((k >> 2) & 1) * 2 + (k >> 3)
            outs[core][k & 3, y, first : first + block.shape[0]] = block

        return store

    feature_grads(low_acts, in3, store_at(768))
    dqkv_in.wait()
    unpack_heads(dqkv, acts)
    wait_all(in1_in)
    feature_grads(acts, in1, store_at(0))


def qkv_grad(dqkv, low, rows1, rows3):
    return kernel_call(
        qkv_grad_kernel,
        (shape_of(4, 4, 1024, 128),) * 2,
        (dqkv, low, *rows1, *rows3),
        [
            pltpu.VMEM((16, 3, 128, 128), bf16),
            pltpu.VMEM((16, 128, 128), bf16),
            pltpu.VMEM((2, 512, 768), bf16),
            pltpu.VMEM((2, 512, 256), bf16),
            ROWS,
            ROWS,
        ],
        12,
        10,
        "qkv_grad",
    )


def visible_end(ends_ref, first):
    places = first + lax.broadcasted_iota(jnp.int32, (1, TILE), 1)
    end = jnp.full((1, TILE), SEQ, jnp.int32)
    for j in range(10, -1, -1):
        end = jnp.where(places < ends_ref[j], ends_ref[j], end)
    return end


def key_blocks(i):
    return min(i + 2, SEQ // TILE)


def rows_of(ref, kind, i):
    return ref[2 * i : 2 * i + 2, kind].reshape(TILE, HEAD_DIM)


def masked(scores, end, kb):
    places = kb * TILE + lax.broadcasted_iota(jnp.int32, (TILE, TILE), 0)
    return jnp.where(places < end, scores, masked_score)


def attend_kernel(ends_ref, qkv_ref, low_ref, out_ref, lse_ref, score_ref, value_ref):
    for i in range(SEQ // TILE):
        value_ref[:, i * TILE : (i + 1) * TILE] = rows_of(qkv_ref, 2, i).astype(f32).T.astype(bf16)
    for i in range(SEQ // TILE):
        query = rows_of(qkv_ref, 0, i)
        end = visible_end(ends_ref, i * TILE)
        top = jnp.full((8, TILE), masked_score, f32)
        for kb in range(key_blocks(i)):
            scores = dot_nt(rows_of(qkv_ref, 1, kb), query) * (score_scale * log2_e)
            if kb >= i:
                scores = masked(scores, end, kb)
            score_ref[kb * TILE : (kb + 1) * TILE, :] = scores
            top = jnp.maximum(top, jnp.max(scores.reshape(TILE // 8, 8, TILE), axis=0))
        top = jnp.max(top, axis=0, keepdims=True)
        total = jnp.zeros((8, TILE), f32)
        acc = jnp.zeros((HEAD_DIM, TILE), f32)
        for kb in range(key_blocks(i)):
            weights = jnp.exp2(score_ref[kb * TILE : (kb + 1) * TILE, :] - top)
            total = total + jnp.sum(weights.reshape(TILE // 8, 8, TILE), axis=0)
            acc = acc + dot_nn(value_ref[:, kb * TILE : (kb + 1) * TILE], weights.astype(bf16))
        total = jnp.sum(total, axis=0, keepdims=True)
        attended = (acc / total).T
        out_ref[i * TILE : (i + 1) * TILE, :] = attended
        low_ref[2 * i : 2 * i + 2] = attended.astype(bf16).reshape(2, 128, HEAD_DIM)
        lse_ref[:, i * TILE : (i + 1) * TILE] = top + jnp.log2(total)


def attend(ends, qkv):
    return pl.pallas_call(
        attend_kernel,
        out_shape=(
            jax.ShapeDtypeStruct((16, 128, HEAD_DIM), bf16),
            jax.ShapeDtypeStruct((SEQ, HEAD_DIM), f32),
            jax.ShapeDtypeStruct((1, SEQ), f32),
        ),
        in_specs=[smem_spec(), vmem_spec()],
        out_specs=(vmem_spec(),) * 3,
        scratch_shapes=[pltpu.VMEM((SEQ, TILE), f32), pltpu.VMEM((HEAD_DIM, SEQ), bf16)],
        compiler_params=params(),
        cost_estimate=cost(8),
        name="attend",
    )(ends, qkv)


def attend_back_kernel(
    ends_ref, qkv_ref, grad_ref, out_ref, lse_ref, cos_ref, sin_ref, dqkv_ref, dk_ref, dv_ref
):
    dk_ref[...] = jnp.zeros_like(dk_ref)
    dv_ref[...] = jnp.zeros_like(dv_ref)

    def turn_back(gradient, i):
        here = slice(i * TILE, (i + 1) * TILE)
        gradient = gradient * score_scale
        turned = gradient * cos_ref[here, :] - pltpu.roll(gradient, 64, 1) * sin_ref[here, :]
        return turned.astype(bf16).reshape(2, 128, HEAD_DIM)

    for i in range(SEQ // TILE):
        here = slice(i * TILE, (i + 1) * TILE)
        query = rows_of(qkv_ref, 0, i)
        grad = grad_ref[2 * i : 2 * i + 2].reshape(TILE, HEAD_DIM)
        product = jnp.sum(grad.astype(f32) * out_ref[here, :], axis=1, keepdims=True)
        delta = jnp.broadcast_to(product, (TILE, 128)).T[0:1, :]
        lse = lse_ref[:, here]
        end = visible_end(ends_ref, i * TILE)
        dq = jnp.zeros((TILE, HEAD_DIM), f32)
        for kb in range(key_blocks(i)):
            there = slice(kb * TILE, (kb + 1) * TILE)
            key = rows_of(qkv_ref, 1, kb)
            scores = dot_nt(key, query) * (score_scale * log2_e)
            if kb >= i:
                scores = masked(scores, end, kb)
            probs = jnp.exp2(scores - lse)
            dv_ref[there, :] += dot_nn(probs.astype(bf16), grad)
            dprobs = dot_nt(rows_of(qkv_ref, 2, kb), grad)
            dscores = (probs * (dprobs - delta)).astype(bf16)
            dk_ref[there, :] += dot_nn(dscores, query)
            dq = dq + dot_tn(dscores, key)
        dqkv_ref[2 * i : 2 * i + 2, 0] = turn_back(dq, i)
    for i in range(SEQ // TILE):
        here = slice(i * TILE, (i + 1) * TILE)
        dqkv_ref[2 * i : 2 * i + 2, 1] = turn_back(dk_ref[here, :], i)
        dqkv_ref[2 * i : 2 * i + 2, 2] = dv_ref[here, :].astype(bf16).reshape(2, 128, HEAD_DIM)


def attend_back(ends, qkv, grad, out, lse, cosine, sine):
    return pl.pallas_call(
        attend_back_kernel,
        out_shape=jax.ShapeDtypeStruct((16, 3, 128, HEAD_DIM), bf16),
        in_specs=[smem_spec()] + [vmem_spec()] * 6,
        out_specs=vmem_spec(),
        scratch_shapes=[pltpu.VMEM((SEQ, HEAD_DIM), f32), pltpu.VMEM((SEQ, HEAD_DIM), f32)],
        compiler_params=params(),
        cost_estimate=cost(15),
        name="attend_back",
    )(ends, qkv, grad, out, lse, cosine, sine)


PLANE = ("yl", "yh", "z")


def plane_exchange(value):
    return lax.all_to_all(value, PLANE, split_axis=0, concat_axis=0, tiled=True)


def rotary(count):
    places = jnp.arange(count, dtype=jnp.int32).astype(f32)
    within = jnp.arange(HEAD_DIM, dtype=jnp.int32) % (HEAD_DIM // 2)
    inverse_freq = 10000.0 ** (within.astype(f32) * (-2.0 / HEAD_DIM))
    angles = places[:, None] * inverse_freq[None, :]
    sign = jnp.where(jnp.arange(HEAD_DIM) < HEAD_DIM // 2, -1.0, 1.0).astype(f32)
    return jnp.cos(angles), jnp.sin(angles) * sign


def inverse_rms(values):
    return lax.rsqrt(jnp.mean(values * values, axis=-1, keepdims=True) + norm_eps)


def norm_back(grad_normed, values, inverse, gain):
    scaled = grad_normed * gain
    gain_part = jnp.sum(grad_normed * values * inverse, axis=0)
    inner = jnp.mean(scaled * values, axis=-1, keepdims=True)
    return inverse * scaled - values * inverse**3 * inner, gain_part


def on_device(
    tokens,
    block_lengths,
    attn_gain,
    query_weight,
    key_weight,
    value_weight,
    out_weight,
    mlp_gain,
    gate_weight,
    up_weight,
    down_weight,
    output_grad,
):
    x, yl, yh, z, c = (lax.axis_index(name) for name in ("x", "yl", "yh", "z", "c"))
    blk = (yh * 4 + z) * 2 + c
    rel = jnp.arange(16, dtype=jnp.int32)
    place = ((yh ^ ((rel >> 2) & 1)) * 4 + (z ^ (rel & 3))) * 2 + (c ^ (rel >> 3))
    chosen = place[:, None] == rel[None, :]

    def relative(gain):
        return jnp.sum(jnp.where(chosen[:, :, None], gain.reshape(1, 16, 128), 0.0), axis=1)

    def absolute(gain):
        return jnp.sum(jnp.where(chosen[:, :, None], gain.reshape(16, 1, 128), 0.0), axis=0)

    first_gain = relative(attn_gain).reshape(1, 2048)
    second_gain = relative(mlp_gain).reshape(1, 2048)
    cosine, sine = rotary(SEQ)
    own_cosine = lax.dynamic_slice_in_dim(cosine, blk * 128, 128, 0)
    own_sine = lax.dynamic_slice_in_dim(sine, blk * 128, 128, 0)
    sequence = (x ^ (blk >> 2)) * 2 + yl
    ends = jnp.cumsum(lax.dynamic_slice_in_dim(block_lengths, sequence, 1, 0)[0])

    normed1, tok_low, dy = prepare(place, tokens[0], output_grad[0], first_gain)
    tok = tok_low.astype(f32)
    blkaxes = ("yh", "z", "c")

    def exchange(value):
        return lax.all_to_all(value, blkaxes, split_axis=0, concat_axis=0, tiled=True)

    shard1 = jnp.concatenate(
        [query_weight.T, key_weight.T, value_weight.T, out_weight], axis=0
    )
    shard_a = jnp.concatenate([gate_weight.T, up_weight.T[:336]], axis=0)
    shard_b = jnp.concatenate([up_weight.T[336:], down_weight], axis=0)
    source = ((yl ^ (rel >> 3)) * 2 + (yh ^ ((rel >> 2) & 1))) * 4 + (z ^ (rel & 3))

    rows1 = gather4(normed1, "x")
    dy_rows = gather4(after(dy, rows1[4]), "x")
    mine = plane_exchange(jnp.broadcast_to(shard1[None], (16,) + shard1.shape))
    mine = after(mine, *rows1[2:4], *dy_rows[2:4], cosine, sine)
    w_attn = (mine, swap(mine, "c", 1))

    orders = "zy", "yz"
    shards = after(shard_a, mine), after(shard_b, mine)
    near = [[swap(v, o[0], 1), swap(v, o[0], 3)] for v, o in zip(shards, orders)]
    rows1 = (after(rows1[0], *near[0], *near[1]),) + rows1[1:]
    far = [swap(n[1], o[0], 1) for n, o in zip(near, orders)]
    qkv = exchange(after(project_qkv(source, rows1, w_attn, own_cosine, own_sine), *far))
    plane = [stacked((v, n[0], f, n[1])) for v, n, f in zip(shards, near, far)]
    tok_rows = gather4(after(tok_low, mine), "x")
    low, attended, lse = attend(ends, after(qkv, *plane, *tok_rows[2:4]))
    low = exchange(low)
    near = [[swap(v, o[1], 1), swap(v, o[1], 3)] for v, o in zip(plane, orders)]
    part = project_out(source, after(low, *near[0], *near[1]), w_attn)
    residual = tok + scatter4([[part[k]] for k in range(4)], "x")
    groups = [gather_far(v, n, o[1]) for v, n, o in zip(plane, near, orders)]
    w_mlp = []
    for group in groups:
        held = [after(piece, residual) for piece in group]
        w_mlp += [*group, *(swap(piece, "c", 1) for piece in held)]
    inverse2 = inverse_rms(residual)
    normed2 = (residual * inverse2 * second_gain).astype(bf16)
    rows2 = gather4(normed2, "x")
    hidden, d_gate, d_up, part = mlp(rows2, dy_rows, w_mlp)

    far = scatter_far([part[2]], "x")
    near1, near3 = scatter_near([part[1]], [part[3]], far, "x")
    mlp_mine, mlp_theirs = mlp_grad(after(d_gate, *far), d_up, hidden, rows2, dy_rows)
    d_normed2 = add(part[0], after(near1, mlp_mine), near3)
    back2, second_part = norm_back(d_normed2, residual, inverse2, second_gain)
    d_residual = dy.astype(f32) + back2
    d_attn = d_residual.astype(bf16)
    rows3 = gather4(d_attn, "x")

    mlp_got = swap(after(mlp_theirs, d_attn), "c", 1)
    rows3 = (after(rows3[0], mlp_got),) + rows3[1:]
    d_out = out_back(source, rows3, w_attn)
    mlp_mine = after(mlp_mine, d_out)
    sums = far_sums(pairs(mlp_mine, mlp_got)[2])
    d_out = exchange(d_out)
    d_out = after(d_out, *sums)
    far = swap(sums[0], "y", 1), swap(sums[1], "y", 3)
    dqkv = attend_back(ends, qkv, d_out, attended, lse, cosine, sine)
    terms = pairs(after(mlp_mine, dqkv), mlp_got)
    sums = near_sums(terms[1], terms[3], far)
    down_part = project_down(after(hidden, dqkv), w_mlp)
    dqkv = exchange(dqkv)
    dqkv = after(dqkv, *sums, down_part)
    near = swap(sums[0], "y", 1), swap(sums[1], "y", 3)

    qkv_mine, qkv_theirs = qkv_grad(dqkv, low, rows1, rows3)
    qkv_got = swap(qkv_theirs, "c", 1)
    part, first_part = qkv_back(source, after(dqkv, qkv_mine), w_attn, tok_rows)
    sums = far_sums(pairs(qkv_mine, qkv_got)[2])
    qkv_far = swap(sums[0], "z", 1), swap(sums[1], "z", 3)
    part = after(part, *sums)
    far = scatter_far([part[2]], "x")
    qkv_terms = pairs(after(qkv_mine, *far), qkv_got)
    sums = near_sums(qkv_terms[1], qkv_terms[3], qkv_far)
    qkv_near = swap(sums[0], "z", 1), swap(sums[1], "z", 3)
    d_near = scatter_near([part[1]], [part[3]], far, "x", sums[:1])
    d_normed1 = add(part[0], *d_near)
    down_part = after(down_part, *sums)
    output = residual + scatter4([[down_part[k]] for k in range(4)], "x")
    layer_output = restore(place, output.astype(bf16))[None]
    back1, _ = norm_back(d_normed1, tok, inverse_rms(tok), first_gain)
    input_grad = d_residual + back1
    along = add(*terms[0], *(after(v, *sums) for v in near)).astype(bf16)
    grad_mlp = scatter4([[along[k]] for k in range(4)], "z")
    along = add(*qkv_terms[0], *qkv_near).astype(bf16)
    grad_qkv = scatter4([[along[k]] for k in range(4)], "y")

    first_part = jnp.sum(after(first_part, *sums), axis=0)
    gains = jnp.concatenate([absolute(first_part), absolute(second_part)], axis=0)
    gains = total4(total4(gains, "x"), "y")
    gains = total4(after(gains, input_grad, *qkv_near), "z")
    gains = gains + swap(gains, "c", 1)
    input_grad = restore(place, input_grad)[None]
    return (
        layer_output,
        input_grad,
        gains[:16].reshape(2048),
        grad_qkv[:256].T,
        grad_qkv[256:512].T,
        grad_qkv[512:768].T,
        grad_qkv[768:],
        gains[16:].reshape(2048),
        grad_mlp[:688].T,
        grad_mlp[688:1376].T,
        grad_mlp[1376:],
    )


def solution(mesh):
    fine = Mesh(mesh.devices.reshape(4, 2, 2, 4, 2), ("x", "yl", "yh", "z", "c"))
    head, blk = ("x", "yl"), ("yh", "z", "c")
    rows = P(head, blk, None)
    wide, tall = P(blk, head), P(head, blk)
    return jax.shard_map(
        on_device,
        mesh=fine,
        in_specs=(rows, P(), P(), wide, wide, wide, tall, P(), wide, wide, tall, rows),
        out_specs=(rows, rows, P(), wide, wide, wide, tall, P(), wide, wide, tall),
        check_vma=False,
    )
```

```python
import functools

import jax
import jax.numpy as jnp
from jax import lax
from jax.experimental import pallas as pl
from jax.experimental.pallas import tpu as pltpu
from jax.sharding import Mesh
from jax.sharding import PartitionSpec as P

HEAD_DIM = 128
SEQ = 2048
TILE = 256
norm_eps = 1e-05
masked_score = -1e30
score_scale = HEAD_DIM ** (-0.5)
log2_e = 1.4426950408889634
f32 = jnp.float32
bf16 = jnp.bfloat16
VMEM_LIMIT = 56 * 1024 * 1024

Y_STEP = {1: 2, 2: 1, 3: 3}


def swap(value, axis, step):
    if axis == "y":
        names, count, step = ("yl", "yh"), 4, Y_STEP[step]
    else:
        names, count = axis, lax.axis_size(axis)
    return lax.ppermute(value, names, [(i, i ^ step) for i in range(count)])


def middle(rows):
    return (rows // 2 + 15) // 16 * 16


def gather4(value, axis, hold=()):
    near = swap(value, axis, 1), swap(value, axis, 3)
    return gather_far(value, near, axis, hold)


def gather_far(value, near, axis, hold=()):
    half = middle(value.shape[0]) if value.ndim == 2 else value.shape[0] // 2
    near1, near3 = near
    far1 = swap(after(near3[:half], *hold), axis, 1)
    return value, near1, far1, swap(near1[half:], axis, 3), near3


def spread4(value, axis):
    return (value, *(swap(value, axis, step) for step in (1, 2, 3)))


def collect4(parts, axis, earlier=()):
    own = parts[0]
    sums = [add(*terms).astype(bf16) for terms in parts[1:]]
    return add(*own, *(swap(after(v, *earlier), axis, k + 1) for k, v in enumerate(sums)))


def add(*values):
    return functools.reduce(lambda a, b: a + b, [value.astype(f32) for value in values])


def after(value, *earlier):
    return lax.optimization_barrier((value, *earlier))[0] if earlier else value


def far_sums(part2):
    rows = part2[0].shape[0]
    half = middle(rows) if part2[0].ndim == 2 else rows // 2
    return (
        add(*[term[:half] for term in part2]).astype(bf16),
        add(*[term[half:] for term in part2]).astype(bf16),
    )


def scatter_far(part2, axis):
    far_a, far_b = far_sums(part2)
    return swap(far_a, axis, 1), swap(far_b, axis, 3)


def near_sums(part1, part3, far):
    from1, from3 = far
    half = from1.shape[0]
    part1 = jnp.concatenate(
        [
            add(*[term[:half] for term in part1]).astype(bf16),
            add(from3, *[term[half:] for term in part1]).astype(bf16),
        ],
        axis=0,
    )
    part3 = jnp.concatenate(
        [
            add(from1, *[term[:half] for term in part3]).astype(bf16),
            add(*[term[half:] for term in part3]).astype(bf16),
        ],
        axis=0,
    )
    return part1, part3


def scatter_near(part1, part3, far, axis, hold=()):
    part1, part3 = near_sums(part1, part3, far)
    return swap(after(part1, *hold), axis, 1), swap(part3, axis, 3)


def scatter4(parts, axis):
    own, part1, part2, part3 = parts
    return add(*scatter_near(part1, part3, scatter_far(part2, axis), axis), *own)


def pairs(mine, got):
    return [[mine[k], got[k]] for k in range(4)]


def total4(value, axis):
    return (value + swap(value, axis, 1)) + (swap(value, axis, 2) + swap(value, axis, 3))


def vmem_spec():
    return pl.BlockSpec(memory_space=pltpu.VMEM)


def smem_spec():
    return pl.BlockSpec(memory_space=pltpu.SMEM)


def params():
    return pltpu.CompilerParams(vmem_limit_bytes=VMEM_LIMIT)


def block_at(place_ref, index):
    return pl.ds(pl.multiple_of(place_ref[index] * 128, 128), 128)


def prepare_kernel(place_ref, tok_ref, dy_ref, gain_ref, h1_ref, tok_out, dy_out):
    total = jnp.zeros((128, 128), f32)
    for r in range(16):
        part = tok_ref[:, r * 128 : (r + 1) * 128].astype(f32)
        total = total + part * part
    inverse = lax.rsqrt(jnp.sum(total, axis=1, keepdims=True) / 2048.0 + norm_eps)
    for r in range(16):
        here = slice(r * 128, (r + 1) * 128)
        there = block_at(place_ref, r)
        part = tok_ref[:, there]
        tok_out[:, here] = part
        dy_out[:, here] = dy_ref[:, there]
        h1_ref[:, here] = (part.astype(f32) * inverse * gain_ref[:, here]).astype(bf16)


def prepare(place, tok, dy, gain):
    out = jax.ShapeDtypeStruct((128, 2048), bf16)
    return pl.pallas_call(
        prepare_kernel,
        out_shape=(out, out, out),
        in_specs=[smem_spec(), vmem_spec(), vmem_spec(), vmem_spec()],
        out_specs=(vmem_spec(),) * 3,
        compiler_params=params(),
        cost_estimate=cost(2.5),
        name="prepare",
    )(place, tok, dy, gain)


def restore_kernel(place_ref, in_ref, out_ref):
    for r in range(16):
        out_ref[:, block_at(place_ref, r)] = in_ref[:, r * 128 : (r + 1) * 128]


def restore(place, value):
    return pl.pallas_call(
        restore_kernel,
        out_shape=jax.ShapeDtypeStruct(value.shape, value.dtype),
        in_specs=[smem_spec(), vmem_spec()],
        out_specs=vmem_spec(),
        compiler_params=params(),
        cost_estimate=cost(2),
        name="restore",
    )(place, value)


def dot_nt(left, right):
    return lax.dot_general(left, right, (((1,), (1,)), ((), ())), preferred_element_type=f32)


def dot_nn(left, right):
    return lax.dot_general(left, right, (((1,), (0,)), ((), ())), preferred_element_type=f32)


def dot_tn(left, right):
    return lax.dot_general(left, right, (((0,), (0,)), ((), ())), preferred_element_type=f32)


def any_spec():
    return pl.BlockSpec(memory_space=pl.ANY)


def pieces_of(order):
    found = []
    for core in range(2):
        for second in range(4):
            for first in range(4):
                z, y = (first, second) if order == "zy" else (second, first)
                slab, turn = y & 1, y >> 1
                if second == 2:
                    array, entry = (2, first) if first < 2 else (3, first - 2)
                else:
                    array, entry = {0: 0, 1: 1, 3: 4}[second], first
                found.append((core * 5 + array, entry, slab, core * 8 + turn * 4 + z))
    return found


GROUP_A, GROUP_B = 1024, 1040
MLP_ROWS = {
    "gate": ((0, 0, 688, 0),),
    "up": ((0, 688, 336, 0), (1, 0, 352, 336)),
    "down": ((1, 352, 688, 0),),
}


class Loader:
    def __init__(self, sems, source_ref=None):
        self.sems = sems
        self.source_ref = source_ref
        self.used = 0

    def copy(self, source, target):
        made = pltpu.make_async_copy(source, target, self.sems.at[self.used])
        self.used += 1
        made.start()
        return made

    def weight(self, refs, first_row, target, source_ref=None):
        source_ref = self.source_ref if source_ref is None else source_ref
        waits = ([], [])
        rows = target.shape[1]
        for core in range(2):
            for k in range(16):
                slab, block = k >> 3, core * 8 + (k & 7)
                waits[slab].append(
                    self.copy(
                        refs[core].at[source_ref[k], first_row : first_row + rows],
                        target.at[slab, :, block * 128 : (block + 1) * 128],
                    )
                )
        return waits

    def mlp_weight(self, pieces, name, target):
        waits = ([], [])
        for group, first_row, rows, at in MLP_ROWS[name]:
            refs = pieces[group * 10 : group * 10 + 10]
            for array, entry, slab, block in pieces_of(("zy", "yz")[group]):
                waits[slab].append(
                    self.copy(
                        refs[array].at[entry, first_row : first_row + rows],
                        target.at[slab, at : at + rows, block * 128 : (block + 1) * 128],
                    )
                )
        return waits

    def rows(self, refs, target):
        copies, first = [], 0
        for ref in refs:
            copies.append(self.copy(ref, target.at[first : first + ref.shape[0]]))
            first += ref.shape[0]
        return copies


def wait_all(copies):
    for made in copies:
        made.wait()


def cost(micros):
    return pl.CostEstimate(flops=int(micros * 1.15e9), bytes_accessed=0, transcendentals=0)


def kernel_call(kernel, out_shape, args, scratch, copies, micros, name, smem=0):
    specs = [any_spec()] * (len(args) - smem)
    return pl.pallas_call(
        kernel,
        out_shape=out_shape,
        in_specs=[smem_spec()] * smem + specs,
        out_specs=jax.tree.map(lambda _: vmem_spec(), out_shape),
        scratch_shapes=list(scratch) + [pltpu.SemaphoreType.DMA((copies,))],
        compiler_params=params(),
        cost_estimate=cost(micros),
        name=name,
    )(*args)


def shape_of(*dims, dtype=bf16):
    return jax.ShapeDtypeStruct(dims, dtype)


ROWS = pltpu.VMEM((512, 2048), bf16)


def weight_scratch(rows):
    return pltpu.VMEM((2, rows, 2048), bf16)


def stack_kernel(own, near1, far, near3, out_ref, sems):
    load = Loader(sems)
    wait_all([load.copy(ref, out_ref.at[n]) for n, ref in enumerate((own, near1, far, near3))])


def stacked(parts):
    own = parts[0]
    return pl.pallas_call(
        stack_kernel,
        out_shape=shape_of(4, *own.shape),
        in_specs=[any_spec()] * 4,
        out_specs=vmem_spec(),
        scratch_shapes=[pltpu.SemaphoreType.DMA((4,))],
        compiler_params=params(),
        cost_estimate=cost(2.5),
        name="stack",
    )(*parts)


def qkv_kernel(source_ref, *refs):
    rows, weights = refs[:5], refs[5:7]
    cos_ref, sin_ref, out_ref, acts, weight, tables, sems = refs[7:]
    load = Loader(sems, source_ref)
    small = [load.copy(cos_ref, tables.at[0]), load.copy(sin_ref, tables.at[1])]
    acts_in = load.rows(rows, acts)
    arrived = load.weight(weights, 0, weight)
    wait_all(small + acts_in)
    for slab in range(2):
        wait_all(arrived[slab])
        for kind in range(3):
            pre = dot_nt(acts[...], weight[slab, kind * 256 : (kind + 1) * 256])
            for head in range(2):
                for j in range(4):
                    tile = pre[j * 128 : (j + 1) * 128, head * 128 : (head + 1) * 128]
                    if kind < 2:
                        tile = tile * tables[0] + pltpu.roll(tile, 64, 1) * tables[1]
                    out_ref[j * 4 + slab * 2 + head, kind] = tile.astype(bf16)


def project_qkv(source, rows, weights, cosine, sine):
    return kernel_call(
        qkv_kernel,
        shape_of(16, 3, 128, 128),
        (source, *rows, *weights, cosine, sine),
        [ROWS, weight_scratch(768), pltpu.VMEM((2, 128, 128), f32)],
        7 + 32,
        10,
        "project_qkv",
        smem=1,
    )


def out_kernel(source_ref, low_ref, mine_ref, theirs_ref, part_ref, low, acts, weight, sems):
    load = Loader(sems, source_ref)
    low_in = load.copy(low_ref, low)
    arrived = load.weight((mine_ref, theirs_ref), 768, weight)
    low_in.wait()
    for p in range(16):
        j, slab, head = p >> 2, (p >> 1) & 1, p & 1
        acts[slab, j * 128 : (j + 1) * 128, head * 128 : (head + 1) * 128] = low[p]
    wait_all(arrived[0] + arrived[1])
    for j in range(0, 4, 2):
        here = slice(j * 128, (j + 2) * 128)
        part = dot_nn(acts[0, here], weight[0]) + dot_nn(acts[1, here], weight[1])
        part_ref[j : j + 2] = part.astype(bf16).reshape(2, 128, 2048)


def project_out(source, low, weights):
    return kernel_call(
        out_kernel,
        shape_of(4, 128, 2048),
        (source, low, *weights),
        [
            pltpu.VMEM((16, 128, 128), bf16),
            pltpu.VMEM((2, 512, 256), bf16),
            weight_scratch(256),
        ],
        1 + 32,
        5,
        "project_out",
        smem=1,
    )


def mlp_kernel(*refs):
    rows, dy_rows, weights = refs[:5], refs[5:9], refs[9:29]
    hidden_ref, d_gate_ref, d_up_ref, part_ref = refs[29:33]
    acts, acts_dy, w_gate, w_up, w_down, acc, sems = refs[33:]
    load = Loader(sems)
    acts_in = load.rows(rows, acts)
    gates = load.mlp_weight(weights, "gate", w_gate)
    ups = load.mlp_weight(weights, "up", w_up)
    dy_in = load.rows(dy_rows, acts_dy)
    downs = load.mlp_weight(weights, "down", w_down)
    wait_all(acts_in)
    for slab in range(2):
        wait_all(gates[slab])
        gate = dot_nt(acts[...], w_gate[slab])
        wait_all(ups[slab])
        up = dot_nt(acts[...], w_up[slab])
        if slab == 0:
            wait_all(dy_in)
        wait_all(downs[slab])
        d_hidden = dot_nt(acts_dy[...], w_down[slab])
        sigmoid = 1.0 / (1.0 + jnp.exp(-gate))
        silu = gate * sigmoid
        hidden_ref[slab] = (silu * up).astype(bf16)
        d_gate_ref[slab] = (d_hidden * up * sigmoid * (1.0 + gate * (1.0 - sigmoid))).astype(bf16)
        d_up_ref[slab] = (d_hidden * silu).astype(bf16)
        part = dot_nn(d_gate_ref[slab], w_gate[slab]) + dot_nn(d_up_ref[slab], w_up[slab])
        if slab == 0:
            acc[...] = part
        else:
            part_ref[...] = (acc[...] + part).astype(bf16).reshape(4, 128, 2048)


def mlp(rows, dy_rows, weights):
    return kernel_call(
        mlp_kernel,
        (shape_of(2, 512, 688),) * 3 + (shape_of(4, 128, 2048),),
        (*rows, *dy_rows, *weights),
        [ROWS, ROWS]
        + [weight_scratch(688)] * 3
        + [pltpu.VMEM((512, 2048), f32)],
        10 + 128,
        28,
        "mlp",
    )


def down_kernel(hidden_ref, *refs):
    weights, (part_ref, hidden, weight, sems) = refs[:20], refs[20:]
    load = Loader(sems)
    hidden_in = load.copy(hidden_ref, hidden)
    arrived = load.mlp_weight(weights, "down", weight)
    hidden_in.wait()
    wait_all(arrived[0] + arrived[1])
    part = dot_nn(hidden[0], weight[0]) + dot_nn(hidden[1], weight[1])
    part_ref[...] = part.astype(bf16).reshape(4, 128, 2048)


def project_down(hidden, weights):
    return kernel_call(
        down_kernel,
        shape_of(4, 128, 2048),
        (hidden, *weights),
        [pltpu.VMEM((2, 512, 688), bf16), weight_scratch(688)],
        1 + 32,
        8,
        "project_down",
    )


def feature_grads(acts, rows, store):
    for slab in range(2):
        for quarter in range(4):
            value = dot_tn(acts[slab], rows[:, quarter * 512 : (quarter + 1) * 512])
            core, turn = divmod(quarter, 2)
            for z in range(4):
                block = value[:, z * 128 : (z + 1) * 128].astype(bf16)
                store(core, slab * 8 + turn * 4 + z, block)


def mlp_grad_kernel(d_gate_ref, d_up_ref, hidden_ref, *refs):
    rows, dy_rows, outs = refs[:5], refs[5:9], (refs[9:11], refs[11:13])
    acts, acts_dy, hidden, sems = refs[13:]
    load = Loader(sems)
    acts_in = load.rows(rows, acts)
    hidden_in = [
        load.copy(ref, hidden.at[n]) for n, ref in enumerate((d_gate_ref, d_up_ref, hidden_ref))
    ]
    dy_in = load.rows(dy_rows, acts_dy)
    wait_all(acts_in)
    for n, name in enumerate(("gate", "up", "down")):
        hidden_in[n].wait()
        if n == 2:
            wait_all(dy_in)

        def store(core, k, block, name=name):
            y, z = ((k >> 2) & 1) * 2 + (k >> 3), k & 3
            for group, first_row, rows, at in MLP_ROWS[name]:
                place = outs[group][core].at[(y, z) if group == 0 else (z, y)]
                place[first_row : first_row + rows] = block[at : at + rows]

        feature_grads(hidden.at[n], acts if n < 2 else acts_dy, store)


def mlp_grad(d_gate, d_up, hidden, rows, dy_rows):
    return kernel_call(
        mlp_grad_kernel,
        (shape_of(4, 4, GROUP_A, 128),) * 2 + (shape_of(4, 4, GROUP_B, 128),) * 2,
        (d_gate, d_up, hidden, *rows, *dy_rows),
        [ROWS, ROWS, pltpu.VMEM((3, 2, 512, 688), bf16)],
        13,
        18,
        "mlp_grad",
    )


def out_back_kernel(source_ref, *refs):
    rows, weights = refs[:5], refs[5:7]
    out_ref, acts, weight, sems = refs[7:]
    load = Loader(sems, source_ref)
    acts_in = load.rows(rows, acts)
    arrived = load.weight(weights, 768, weight)
    wait_all(acts_in)
    for slab in range(2):
        wait_all(arrived[slab])
        value = dot_nt(acts[...], weight[slab]).astype(bf16)
        for j in range(4):
            for head in range(2):
                out_ref[j * 4 + slab * 2 + head] = value[
                    j * 128 : (j + 1) * 128, head * 128 : (head + 1) * 128
                ]


def out_back(source, rows, weights):
    return kernel_call(
        out_back_kernel,
        shape_of(16, 128, 128),
        (source, *rows, *weights),
        [ROWS, weight_scratch(256)],
        5 + 32,
        6,
        "out_back",
        smem=1,
    )


def unpack_heads(source, target):
    for p in range(16):
        j, slab, head = p >> 2, (p >> 1) & 1, p & 1
        for kind in range(3):
            column = (kind * 2 + head) * 128
            target[slab, j * 128 : (j + 1) * 128, column : column + 128] = source[p, kind]


def qkv_back_kernel(source_ref, dqkv_ref, mine_ref, theirs_ref, *refs):
    part_ref, dqkv, acts, weight, acc, sems = refs
    load = Loader(sems, source_ref)
    dqkv_in = load.copy(dqkv_ref, dqkv)
    arrived = load.weight((mine_ref, theirs_ref), 0, weight)
    dqkv_in.wait()
    unpack_heads(dqkv, acts)
    for slab in range(2):
        wait_all(arrived[slab])
        part = dot_nn(acts[slab], weight[slab])
        if slab == 0:
            acc[...] = part
        else:
            part_ref[...] = (acc[...] + part).astype(bf16).reshape(4, 128, 2048)


def qkv_back(source, dqkv, weights):
    return kernel_call(
        qkv_back_kernel,
        shape_of(4, 128, 2048),
        (source, dqkv, *weights),
        [
            pltpu.VMEM((16, 3, 128, 128), bf16),
            pltpu.VMEM((2, 512, 768), bf16),
            weight_scratch(768),
            pltpu.VMEM((512, 2048), f32),
        ],
        1 + 32,
        9,
        "qkv_back",
        smem=1,
    )


def qkv_grad_kernel(dqkv_ref, low_ref, *refs):
    rows1, rows3, outs = refs[:5], refs[5:10], refs[10:12]
    dqkv, low, acts, low_acts, in1, in3, sems = refs[12:]
    load = Loader(sems)
    low_in = load.copy(low_ref, low)
    in3_in = load.rows(rows3, in3)
    dqkv_in = load.copy(dqkv_ref, dqkv)
    in1_in = load.rows(rows1, in1)
    low_in.wait()
    for p in range(16):
        j, slab, head = p >> 2, (p >> 1) & 1, p & 1
        low_acts[slab, j * 128 : (j + 1) * 128, head * 128 : (head + 1) * 128] = low[p]
    wait_all(in3_in)

    def store_at(first):
        def store(core, k, block):
            y = ((k >> 2) & 1) * 2 + (k >> 3)
            outs[core][k & 3, y, first : first + block.shape[0]] = block

        return store

    feature_grads(low_acts, in3, store_at(768))
    dqkv_in.wait()
    unpack_heads(dqkv, acts)
    wait_all(in1_in)
    feature_grads(acts, in1, store_at(0))


def qkv_grad(dqkv, low, rows1, rows3):
    return kernel_call(
        qkv_grad_kernel,
        (shape_of(4, 4, 1024, 128),) * 2,
        (dqkv, low, *rows1, *rows3),
        [
            pltpu.VMEM((16, 3, 128, 128), bf16),
            pltpu.VMEM((16, 128, 128), bf16),
            pltpu.VMEM((2, 512, 768), bf16),
            pltpu.VMEM((2, 512, 256), bf16),
            ROWS,
            ROWS,
        ],
        12,
        10,
        "qkv_grad",
    )


def visible_end(ends_ref, first):
    places = first + lax.broadcasted_iota(jnp.int32, (1, TILE), 1)
    end = jnp.full((1, TILE), SEQ, jnp.int32)
    for j in range(10, -1, -1):
        end = jnp.where(places < ends_ref[j], ends_ref[j], end)
    return end


def key_blocks(i):
    return min(i + 2, SEQ // TILE)


def rows_of(ref, kind, i):
    return ref[2 * i : 2 * i + 2, kind].reshape(TILE, HEAD_DIM)


def masked(scores, end, kb):
    places = kb * TILE + lax.broadcasted_iota(jnp.int32, (TILE, TILE), 0)
    return jnp.where(places < end, scores, masked_score)


def attend_kernel(ends_ref, qkv_ref, low_ref, out_ref, lse_ref, score_ref, value_ref):
    for i in range(SEQ // TILE):
        value_ref[:, i * TILE : (i + 1) * TILE] = rows_of(qkv_ref, 2, i).astype(f32).T.astype(bf16)
    for i in range(SEQ // TILE):
        query = rows_of(qkv_ref, 0, i)
        end = visible_end(ends_ref, i * TILE)
        top = jnp.full((8, TILE), masked_score, f32)
        for kb in range(key_blocks(i)):
            scores = dot_nt(rows_of(qkv_ref, 1, kb), query) * (score_scale * log2_e)
            if kb >= i:
                scores = masked(scores, end, kb)
            score_ref[kb * TILE : (kb + 1) * TILE, :] = scores
            top = jnp.maximum(top, jnp.max(scores.reshape(TILE // 8, 8, TILE), axis=0))
        top = jnp.max(top, axis=0, keepdims=True)
        total = jnp.zeros((8, TILE), f32)
        acc = jnp.zeros((HEAD_DIM, TILE), f32)
        for kb in range(key_blocks(i)):
            weights = jnp.exp2(score_ref[kb * TILE : (kb + 1) * TILE, :] - top)
            total = total + jnp.sum(weights.reshape(TILE // 8, 8, TILE), axis=0)
            acc = acc + dot_nn(value_ref[:, kb * TILE : (kb + 1) * TILE], weights.astype(bf16))
        total = jnp.sum(total, axis=0, keepdims=True)
        attended = (acc / total).T
        out_ref[i * TILE : (i + 1) * TILE, :] = attended
        low_ref[2 * i : 2 * i + 2] = attended.astype(bf16).reshape(2, 128, HEAD_DIM)
        lse_ref[:, i * TILE : (i + 1) * TILE] = top + jnp.log2(total)


def attend(ends, qkv):
    return pl.pallas_call(
        attend_kernel,
        out_shape=(
            jax.ShapeDtypeStruct((16, 128, HEAD_DIM), bf16),
            jax.ShapeDtypeStruct((SEQ, HEAD_DIM), f32),
            jax.ShapeDtypeStruct((1, SEQ), f32),
        ),
        in_specs=[smem_spec(), vmem_spec()],
        out_specs=(vmem_spec(),) * 3,
        scratch_shapes=[pltpu.VMEM((SEQ, TILE), f32), pltpu.VMEM((HEAD_DIM, SEQ), bf16)],
        compiler_params=params(),
        cost_estimate=cost(8),
        name="attend",
    )(ends, qkv)


def attend_back_kernel(
    ends_ref, qkv_ref, grad_ref, out_ref, lse_ref, cos_ref, sin_ref, dqkv_ref, dk_ref, dv_ref
):
    dk_ref[...] = jnp.zeros_like(dk_ref)
    dv_ref[...] = jnp.zeros_like(dv_ref)

    def turn_back(gradient, i):
        here = slice(i * TILE, (i + 1) * TILE)
        gradient = gradient * score_scale
        turned = gradient * cos_ref[here, :] - pltpu.roll(gradient, 64, 1) * sin_ref[here, :]
        return turned.astype(bf16).reshape(2, 128, HEAD_DIM)

    for i in range(SEQ // TILE):
        here = slice(i * TILE, (i + 1) * TILE)
        query = rows_of(qkv_ref, 0, i)
        grad = grad_ref[2 * i : 2 * i + 2].reshape(TILE, HEAD_DIM)
        product = jnp.sum(grad.astype(f32) * out_ref[here, :], axis=1, keepdims=True)
        delta = jnp.broadcast_to(product, (TILE, 128)).T[0:1, :]
        lse = lse_ref[:, here]
        end = visible_end(ends_ref, i * TILE)
        dq = jnp.zeros((TILE, HEAD_DIM), f32)
        for kb in range(key_blocks(i)):
            there = slice(kb * TILE, (kb + 1) * TILE)
            key = rows_of(qkv_ref, 1, kb)
            scores = dot_nt(key, query) * (score_scale * log2_e)
            if kb >= i:
                scores = masked(scores, end, kb)
            probs = jnp.exp2(scores - lse)
            dv_ref[there, :] += dot_nn(probs.astype(bf16), grad)
            dprobs = dot_nt(rows_of(qkv_ref, 2, kb), grad)
            dscores = (probs * (dprobs - delta)).astype(bf16)
            dk_ref[there, :] += dot_nn(dscores, query)
            dq = dq + dot_tn(dscores, key)
        dqkv_ref[2 * i : 2 * i + 2, 0] = turn_back(dq, i)
    for i in range(SEQ // TILE):
        here = slice(i * TILE, (i + 1) * TILE)
        dqkv_ref[2 * i : 2 * i + 2, 1] = turn_back(dk_ref[here, :], i)
        dqkv_ref[2 * i : 2 * i + 2, 2] = dv_ref[here, :].astype(bf16).reshape(2, 128, HEAD_DIM)


def attend_back(ends, qkv, grad, out, lse, cosine, sine):
    return pl.pallas_call(
        attend_back_kernel,
        out_shape=jax.ShapeDtypeStruct((16, 3, 128, HEAD_DIM), bf16),
        in_specs=[smem_spec()] + [vmem_spec()] * 6,
        out_specs=vmem_spec(),
        scratch_shapes=[pltpu.VMEM((SEQ, HEAD_DIM), f32), pltpu.VMEM((SEQ, HEAD_DIM), f32)],
        compiler_params=params(),
        cost_estimate=cost(15),
        name="attend_back",
    )(ends, qkv, grad, out, lse, cosine, sine)


PLANE = ("yl", "yh", "z")


def plane_exchange(value):
    return lax.all_to_all(value, PLANE, split_axis=0, concat_axis=0, tiled=True)


def rotary(count):
    places = jnp.arange(count, dtype=jnp.int32).astype(f32)
    within = jnp.arange(HEAD_DIM, dtype=jnp.int32) % (HEAD_DIM // 2)
    inverse_freq = 10000.0 ** (within.astype(f32) * (-2.0 / HEAD_DIM))
    angles = places[:, None] * inverse_freq[None, :]
    sign = jnp.where(jnp.arange(HEAD_DIM) < HEAD_DIM // 2, -1.0, 1.0).astype(f32)
    return jnp.cos(angles), jnp.sin(angles) * sign


def inverse_rms(values):
    return lax.rsqrt(jnp.mean(values * values, axis=-1, keepdims=True) + norm_eps)


def norm_back(grad_normed, values, inverse, gain):
    scaled = grad_normed * gain
    gain_part = jnp.sum(grad_normed * values * inverse, axis=0)
    inner = jnp.mean(scaled * values, axis=-1, keepdims=True)
    return inverse * scaled - values * inverse**3 * inner, gain_part


def on_device(
    tokens,
    block_lengths,
    attn_gain,
    query_weight,
    key_weight,
    value_weight,
    out_weight,
    mlp_gain,
    gate_weight,
    up_weight,
    down_weight,
    output_grad,
):
    x, yl, yh, z, c = (lax.axis_index(name) for name in ("x", "yl", "yh", "z", "c"))
    blk = (yh * 4 + z) * 2 + c
    rel = jnp.arange(16, dtype=jnp.int32)
    place = ((yh ^ ((rel >> 2) & 1)) * 4 + (z ^ (rel & 3))) * 2 + (c ^ (rel >> 3))
    chosen = place[:, None] == rel[None, :]

    def relative(gain):
        return jnp.sum(jnp.where(chosen[:, :, None], gain.reshape(1, 16, 128), 0.0), axis=1)

    def absolute(gain):
        return jnp.sum(jnp.where(chosen[:, :, None], gain.reshape(16, 1, 128), 0.0), axis=0)

    first_gain = relative(attn_gain).reshape(1, 2048)
    second_gain = relative(mlp_gain).reshape(1, 2048)
    cosine, sine = rotary(SEQ)
    own_cosine = lax.dynamic_slice_in_dim(cosine, blk * 128, 128, 0)
    own_sine = lax.dynamic_slice_in_dim(sine, blk * 128, 128, 0)
    sequence = (x ^ (blk >> 2)) * 2 + yl
    ends = jnp.cumsum(lax.dynamic_slice_in_dim(block_lengths, sequence, 1, 0)[0])

    normed1, tok, dy = prepare(place, tokens[0], output_grad[0], first_gain)
    tok = tok.astype(f32)
    blkaxes = ("yh", "z", "c")

    def exchange(value):
        return lax.all_to_all(value, blkaxes, split_axis=0, concat_axis=0, tiled=True)

    shard1 = jnp.concatenate(
        [query_weight.T, key_weight.T, value_weight.T, out_weight], axis=0
    )
    shard_a = jnp.concatenate([gate_weight.T, up_weight.T[:336]], axis=0)
    shard_b = jnp.concatenate([up_weight.T[336:], down_weight], axis=0)
    source = ((yl ^ (rel >> 3)) * 2 + (yh ^ ((rel >> 2) & 1))) * 4 + (z ^ (rel & 3))

    rows1 = gather4(normed1, "x")
    dy_rows = spread4(after(dy, rows1[4]), "x")
    mine = plane_exchange(jnp.broadcast_to(shard1[None], (16,) + shard1.shape))
    mine = after(mine, *rows1[2:4], *dy_rows[1:], cosine, sine)
    w_attn = (mine, swap(mine, "c", 1))

    orders = "zy", "yz"
    shards = after(shard_a, mine), after(shard_b, mine)
    pieces = [spread4(v, o[0]) for v, o in zip(shards, orders)]
    qkv = project_qkv(source, rows1, w_attn, own_cosine, own_sine)
    qkv = exchange(after(qkv, *pieces[0], *pieces[1]))
    plane = [stacked(v) for v in pieces]
    low, attended, lse = attend(ends, after(qkv, *plane))
    low = exchange(low)
    near = [[swap(v, o[1], 1), swap(v, o[1], 3)] for v, o in zip(plane, orders)]
    part = project_out(source, after(low, *near[0], *near[1]), w_attn)
    residual = tok + scatter4([[part[k]] for k in range(4)], "x")
    groups = [gather_far(v, n, o[1]) for v, n, o in zip(plane, near, orders)]
    w_mlp = []
    for group in groups:
        held = [after(piece, residual) for piece in group]
        w_mlp += [*group, *(swap(piece, "c", 1) for piece in held)]
    inverse2 = inverse_rms(residual)
    normed2 = (residual * inverse2 * second_gain).astype(bf16)
    rows2 = gather4(normed2, "x")
    hidden, d_gate, d_up, part = mlp(rows2, dy_rows, w_mlp)

    far = scatter_far([part[2]], "x")
    near1, near3 = scatter_near([part[1]], [part[3]], far, "x")
    grads = mlp_grad(after(d_gate, *far), d_up, hidden, rows2, dy_rows)
    d_normed2 = add(part[0], after(near1, grads[0]), near3)
    back2, second_part = norm_back(d_normed2, residual, inverse2, second_gain)
    d_residual = dy.astype(f32) + back2
    d_attn = d_residual.astype(bf16)
    rows3 = gather4(d_attn, "x")

    orders = "yz", "zy"
    mine = grads[0], grads[2]
    got = [swap(after(v, d_attn), "c", 1) for v in (grads[1], grads[3])]
    terms = [pairs(m, g) for m, g in zip(mine, got)]
    sums = [far_sums(t[2]) for t in terms]
    rows3 = (after(rows3[0], *sums[0], *sums[1]),) + rows3[1:]
    far = [(swap(v[0], o[0], 1), swap(v[1], o[0], 3)) for v, o in zip(sums, orders)]
    d_out = out_back(source, rows3, w_attn)
    terms = [pairs(after(m, d_out), g) for m, g in zip(mine, got)]
    sums = [near_sums(t[1], t[3], f) for t, f in zip(terms, far)]
    d_out = exchange(d_out)
    d_out = after(d_out, *sums[0], *sums[1])
    near = [(swap(v[0], o[0], 1), swap(v[1], o[0], 3)) for v, o in zip(sums, orders)]
    dqkv = attend_back(ends, qkv, d_out, attended, lse, cosine, sine)
    dqkv = after(dqkv, *near[0], *near[1])
    down_part = project_down(after(hidden, dqkv), w_mlp)
    out_far = scatter_far([down_part[2]], "x")
    mine = after(mine[0], down_part), after(mine[1], down_part)
    terms = [pairs(m, g) for m, g in zip(mine, got)]
    along = [add(*t[0], *n).astype(bf16) for t, n in zip(terms, near)]
    dqkv = after(exchange(dqkv), *out_far, *along)

    qkv_mine, qkv_theirs = qkv_grad(dqkv, low, rows1, rows3)
    qkv_got = swap(qkv_theirs, "c", 1)
    part = qkv_back(source, after(dqkv, qkv_mine), w_attn)
    sums = far_sums(pairs(qkv_mine, qkv_got)[2])
    qkv_far = swap(sums[0], "z", 1), swap(sums[1], "z", 3)
    part = after(part, *sums)
    far = scatter_far([part[2]], "x")
    qkv_terms = pairs(after(qkv_mine, *far), qkv_got)
    sums = near_sums(qkv_terms[1], qkv_terms[3], qkv_far)
    qkv_near = swap(sums[0], "z", 1), swap(sums[1], "z", 3)
    d_near = scatter_near([part[1]], [part[3]], far, "x")
    d_normed1 = add(part[0], *d_near)
    out_near = scatter_near([after(down_part[1], *d_near)], [down_part[3]], out_far, "x")
    output = residual + add(down_part[0], *out_near)
    layer_output = restore(place, output.astype(bf16))[None]
    back1, first_part = norm_back(d_normed1, tok, inverse_rms(tok), first_gain)
    input_grad = d_residual + back1
    along = [after(v, *sums) for v in along]
    grad_a, grad_b = (
        collect4([[v[k]] for k in range(4)], o[1]) for v, o in zip(along, orders)
    )
    along = add(*qkv_terms[0], *qkv_near).astype(bf16)
    grad_qkv = collect4([[along[k]] for k in range(4)], "y")

    gains = jnp.concatenate([absolute(first_part), absolute(second_part)], axis=0)
    gains = total4(total4(gains, "x"), "y")
    gains = total4(after(gains, *qkv_near), "z")
    gains = gains + swap(gains, "c", 1)
    input_grad = restore(place, input_grad)[None]
    return (
        layer_output,
        input_grad,
        gains[:16].reshape(2048),
        grad_qkv[:256].T,
        grad_qkv[256:512].T,
        grad_qkv[512:768].T,
        grad_qkv[768:],
        gains[16:].reshape(2048),
        grad_a[:688].T,
        jnp.concatenate([grad_a[688:], grad_b[:352]], axis=0).T,
        grad_b[352:],
    )


def solution(mesh):
    fine = Mesh(mesh.devices.reshape(4, 2, 2, 4, 2), ("x", "yl", "yh", "z", "c"))
    head, blk = ("x", "yl"), ("yh", "z", "c")
    rows = P(head, blk, None)
    wide, tall = P(blk, head), P(head, blk)
    return jax.shard_map(
        on_device,
        mesh=fine,
        in_specs=(rows, P(), P(), wide, wide, wide, tall, P(), wide, wide, tall, rows),
        out_specs=(rows, rows, P(), wide, wide, wide, tall, P(), wide, wide, tall),
        check_vma=False,
    )
```

```python
import functools

import jax
import jax.numpy as jnp
from jax import lax
from jax.experimental import pallas as pl
from jax.experimental.pallas import tpu as pltpu
from jax.sharding import Mesh
from jax.sharding import PartitionSpec as P

HEAD_DIM = 128
SEQ = 2048
TILE = 256
norm_eps = 1e-05
masked_score = -1e30
score_scale = HEAD_DIM ** (-0.5)
log2_e = 1.4426950408889634
f32 = jnp.float32
bf16 = jnp.bfloat16
VMEM_LIMIT = 56 * 1024 * 1024

Y_STEP = {1: 2, 2: 1, 3: 3}


def swap(value, axis, step):
    if axis == "y":
        names, count, step = ("yl", "yh"), 4, Y_STEP[step]
    else:
        names, count = axis, lax.axis_size(axis)
    return lax.ppermute(value, names, [(i, i ^ step) for i in range(count)])


def middle(rows):
    return (rows // 2 + 15) // 16 * 16


def gather4(value, axis, hold=()):
    near = swap(value, axis, 1), swap(value, axis, 3)
    return gather_far(value, near, axis, hold)


def gather_far(value, near, axis, hold=()):
    half = middle(value.shape[0]) if value.ndim == 2 else value.shape[0] // 2
    near1, near3 = near
    far1 = swap(after(near3[:half], *hold), axis, 1)
    return value, near1, far1, swap(near1[half:], axis, 3), near3


def spread4(value, axis):
    return (value, *(swap(value, axis, step) for step in (1, 2, 3)))


def collect4(parts, axis, earlier=()):
    own = parts[0]
    sums = [add(*terms).astype(bf16) for terms in parts[1:]]
    return add(*own, *(swap(after(v, *earlier), axis, k + 1) for k, v in enumerate(sums)))


def add(*values):
    return functools.reduce(lambda a, b: a + b, [value.astype(f32) for value in values])


def after(value, *earlier):
    return lax.optimization_barrier((value, *earlier))[0] if earlier else value


def far_sums(part2):
    rows = part2[0].shape[0]
    half = middle(rows) if part2[0].ndim == 2 else rows // 2
    return (
        add(*[term[:half] for term in part2]).astype(bf16),
        add(*[term[half:] for term in part2]).astype(bf16),
    )


def scatter_far(part2, axis):
    far_a, far_b = far_sums(part2)
    return swap(far_a, axis, 1), swap(far_b, axis, 3)


def near_sums(part1, part3, far):
    from1, from3 = far
    half = from1.shape[0]
    part1 = jnp.concatenate(
        [
            add(*[term[:half] for term in part1]).astype(bf16),
            add(from3, *[term[half:] for term in part1]).astype(bf16),
        ],
        axis=0,
    )
    part3 = jnp.concatenate(
        [
            add(from1, *[term[:half] for term in part3]).astype(bf16),
            add(*[term[half:] for term in part3]).astype(bf16),
        ],
        axis=0,
    )
    return part1, part3


def scatter_near(part1, part3, far, axis, hold=()):
    part1, part3 = near_sums(part1, part3, far)
    return swap(after(part1, *hold), axis, 1), swap(part3, axis, 3)


def scatter4(parts, axis):
    own, part1, part2, part3 = parts
    return add(*scatter_near(part1, part3, scatter_far(part2, axis), axis), *own)


def pairs(mine, got):
    return [[mine[k], got[k]] for k in range(4)]


def total4(value, axis):
    return (value + swap(value, axis, 1)) + (swap(value, axis, 2) + swap(value, axis, 3))


def vmem_spec():
    return pl.BlockSpec(memory_space=pltpu.VMEM)


def smem_spec():
    return pl.BlockSpec(memory_space=pltpu.SMEM)


def params():
    return pltpu.CompilerParams(vmem_limit_bytes=VMEM_LIMIT)


def block_at(place_ref, index):
    return pl.ds(pl.multiple_of(place_ref[index] * 128, 128), 128)


def prepare_kernel(place_ref, tok_ref, dy_ref, gain_ref, h1_ref, tok_out, dy_out):
    total = jnp.zeros((128, 128), f32)
    for r in range(16):
        part = tok_ref[:, r * 128 : (r + 1) * 128].astype(f32)
        total = total + part * part
    inverse = lax.rsqrt(jnp.sum(total, axis=1, keepdims=True) / 2048.0 + norm_eps)
    for r in range(16):
        here = slice(r * 128, (r + 1) * 128)
        there = block_at(place_ref, r)
        part = tok_ref[:, there]
        tok_out[:, here] = part
        dy_out[:, here] = dy_ref[:, there]
        h1_ref[:, here] = (part.astype(f32) * inverse * gain_ref[:, here]).astype(bf16)


def prepare(place, tok, dy, gain):
    out = jax.ShapeDtypeStruct((128, 2048), bf16)
    return pl.pallas_call(
        prepare_kernel,
        out_shape=(out, out, out),
        in_specs=[smem_spec(), vmem_spec(), vmem_spec(), vmem_spec()],
        out_specs=(vmem_spec(),) * 3,
        compiler_params=params(),
        cost_estimate=cost(2.5),
        name="prepare",
    )(place, tok, dy, gain)


def share_kernel(query_ref, key_ref, value_ref, out_w_ref, copies_ref, rows, sems):
    for n, ref in enumerate((query_ref, key_ref, value_ref)):
        rows[n * 256 : (n + 1) * 256] = ref[...].astype(f32).T.astype(bf16)
    rows[768:] = out_w_ref[...]
    made = [pltpu.make_async_copy(rows, copies_ref.at[k], sems.at[k]) for k in range(16)]
    for copy in made:
        copy.start()
    for copy in made:
        copy.wait()


def share(query, key, value, out_weight):
    return pl.pallas_call(
        share_kernel,
        out_shape=jax.ShapeDtypeStruct((16, 1024, 128), bf16),
        in_specs=[vmem_spec()] * 4,
        out_specs=pl.BlockSpec(memory_space=pl.ANY),
        scratch_shapes=[pltpu.VMEM((1024, 128), bf16), pltpu.SemaphoreType.DMA((16,))],
        compiler_params=params(),
        cost_estimate=cost(3),
        name="share",
    )(query, key, value, out_weight)


def restore_kernel(place_ref, in_ref, out_ref):
    for r in range(16):
        out_ref[:, block_at(place_ref, r)] = in_ref[:, r * 128 : (r + 1) * 128]


def restore(place, value):
    return pl.pallas_call(
        restore_kernel,
        out_shape=jax.ShapeDtypeStruct(value.shape, value.dtype),
        in_specs=[smem_spec(), vmem_spec()],
        out_specs=vmem_spec(),
        compiler_params=params(),
        cost_estimate=cost(2),
        name="restore",
    )(place, value)


def dot_nt(left, right):
    return lax.dot_general(left, right, (((1,), (1,)), ((), ())), preferred_element_type=f32)


def dot_nn(left, right):
    return lax.dot_general(left, right, (((1,), (0,)), ((), ())), preferred_element_type=f32)


def dot_tn(left, right):
    return lax.dot_general(left, right, (((0,), (0,)), ((), ())), preferred_element_type=f32)


def any_spec():
    return pl.BlockSpec(memory_space=pl.ANY)


def pieces_of(order):
    found = []
    for core in range(2):
        for second in range(4):
            for first in range(4):
                z, y = (first, second) if order == "zy" else (second, first)
                slab, turn = y & 1, y >> 1
                if second == 2:
                    array, entry = (2, first) if first < 2 else (3, first - 2)
                else:
                    array, entry = {0: 0, 1: 1, 3: 4}[second], first
                found.append((core * 5 + array, entry, slab, core * 8 + turn * 4 + z))
    return found


GROUP_A, GROUP_B = 1024, 1040
MLP_ROWS = {
    "gate": ((0, 0, 688, 0),),
    "up": ((0, 688, 336, 0), (1, 0, 352, 336)),
    "down": ((1, 352, 688, 0),),
}


class Loader:
    def __init__(self, sems, source_ref=None):
        self.sems = sems
        self.source_ref = source_ref
        self.used = 0

    def copy(self, source, target):
        made = pltpu.make_async_copy(source, target, self.sems.at[self.used])
        self.used += 1
        made.start()
        return made

    def weight(self, refs, first_row, target, source_ref=None):
        source_ref = self.source_ref if source_ref is None else source_ref
        waits = ([], [])
        rows = target.shape[1]
        for slab in range(2):
            for core in range(2):
                for k in range(8):
                    block = core * 8 + k
                    waits[slab].append(
                        self.copy(
                            refs[core].at[source_ref[slab * 8 + k], first_row : first_row + rows],
                            target.at[slab, :, block * 128 : (block + 1) * 128],
                        )
                    )
        return waits

    def mlp_weight(self, pieces, name, target, slabs=(0, 1)):
        waits = ([], [])
        for group, first_row, rows, at in MLP_ROWS[name]:
            refs = pieces[group * 10 : group * 10 + 10]
            for array, entry, slab, block in pieces_of(("zy", "yz")[group]):
                if slab not in slabs:
                    continue
                waits[slab].append(
                    self.copy(
                        refs[array].at[entry, first_row : first_row + rows],
                        target.at[slab, at : at + rows, block * 128 : (block + 1) * 128],
                    )
                )
        return waits

    def rows(self, refs, target):
        copies, first = [], 0
        for ref in refs:
            copies.append(self.copy(ref, target.at[first : first + ref.shape[0]]))
            first += ref.shape[0]
        return copies


def wait_all(copies):
    for made in copies:
        made.wait()


def cost(micros):
    return pl.CostEstimate(flops=int(micros * 1.15e9), bytes_accessed=0, transcendentals=0)


def kernel_call(kernel, out_shape, args, scratch, copies, micros, name, smem=0):
    specs = [any_spec()] * (len(args) - smem)
    return pl.pallas_call(
        kernel,
        out_shape=out_shape,
        in_specs=[smem_spec()] * smem + specs,
        out_specs=jax.tree.map(lambda _: vmem_spec(), out_shape),
        scratch_shapes=list(scratch) + [pltpu.SemaphoreType.DMA((copies,))],
        compiler_params=params(),
        cost_estimate=cost(micros),
        name=name,
    )(*args)


def shape_of(*dims, dtype=bf16):
    return jax.ShapeDtypeStruct(dims, dtype)


ROWS = pltpu.VMEM((512, 2048), bf16)


def weight_scratch(rows):
    return pltpu.VMEM((2, rows, 2048), bf16)


def stack_kernel(own, near1, far, near3, out_ref, sems):
    load = Loader(sems)
    wait_all([load.copy(ref, out_ref.at[n]) for n, ref in enumerate((own, near1, far, near3))])


def stacked(parts):
    own = parts[0]
    return pl.pallas_call(
        stack_kernel,
        out_shape=shape_of(4, *own.shape),
        in_specs=[any_spec()] * 4,
        out_specs=vmem_spec(),
        scratch_shapes=[pltpu.SemaphoreType.DMA((4,))],
        compiler_params=params(),
        cost_estimate=cost(2.5),
        name="stack",
    )(*parts)


def qkv_kernel(source_ref, *refs):
    rows, weights = refs[:5], refs[5:7]
    cos_ref, sin_ref, out_ref, acts, weight, tables, sems = refs[7:]
    load = Loader(sems, source_ref)
    small = [load.copy(cos_ref, tables.at[0]), load.copy(sin_ref, tables.at[1])]
    acts_in = load.rows(rows, acts)
    arrived = load.weight(weights, 0, weight)
    wait_all(small + acts_in)
    for slab in range(2):
        wait_all(arrived[slab])
        for kind in range(3):
            pre = dot_nt(acts[...], weight[slab, kind * 256 : (kind + 1) * 256])
            for head in range(2):
                for j in range(4):
                    tile = pre[j * 128 : (j + 1) * 128, head * 128 : (head + 1) * 128]
                    if kind < 2:
                        tile = tile * tables[0] + pltpu.roll(tile, 64, 1) * tables[1]
                    out_ref[j * 4 + slab * 2 + head, kind] = tile.astype(bf16)


def project_qkv(source, rows, weights, cosine, sine):
    return kernel_call(
        qkv_kernel,
        shape_of(16, 3, 128, 128),
        (source, *rows, *weights, cosine, sine),
        [ROWS, weight_scratch(768), pltpu.VMEM((2, 128, 128), f32)],
        7 + 32,
        10,
        "project_qkv",
        smem=1,
    )


def out_kernel(source_ref, low_ref, mine_ref, theirs_ref, part_ref, low, acts, weight, sems):
    load = Loader(sems, source_ref)
    low_in = load.copy(low_ref, low)
    arrived = load.weight((mine_ref, theirs_ref), 768, weight)
    low_in.wait()
    for p in range(16):
        j, slab, head = p >> 2, (p >> 1) & 1, p & 1
        acts[slab, j * 128 : (j + 1) * 128, head * 128 : (head + 1) * 128] = low[p]
    wait_all(arrived[0] + arrived[1])
    for j in range(0, 4, 2):
        here = slice(j * 128, (j + 2) * 128)
        part = dot_nn(acts[0, here], weight[0]) + dot_nn(acts[1, here], weight[1])
        part_ref[j : j + 2] = part.astype(bf16).reshape(2, 128, 2048)


def project_out(source, low, weights):
    return kernel_call(
        out_kernel,
        shape_of(4, 128, 2048),
        (source, low, *weights),
        [
            pltpu.VMEM((16, 128, 128), bf16),
            pltpu.VMEM((2, 512, 256), bf16),
            weight_scratch(256),
        ],
        1 + 32,
        5,
        "project_out",
        smem=1,
    )


def mlp_kernel(*refs):
    rows, dy_rows, weights = refs[:5], refs[5:9], refs[9:29]
    hidden_ref, d_gate_ref, d_up_ref, part_ref = refs[29:33]
    acts, acts_dy, w_gate, w_up, w_down, sems = refs[33:]
    load = Loader(sems)
    acts_in = load.rows(rows, acts)
    names = ("gate", w_gate), ("up", w_up), ("down", w_down)
    first = [load.mlp_weight(weights, *name, slabs=(0,))[0] for name in names[:2]]
    dy_in = load.rows(dy_rows, acts_dy)
    first.append(load.mlp_weight(weights, *names[2], slabs=(0,))[0])
    second = [load.mlp_weight(weights, *name, slabs=(1,))[1] for name in names]
    gates, ups, downs = zip(first, second)
    wait_all(acts_in)
    for slab in range(2):
        wait_all(gates[slab])
        gate = dot_nt(acts[...], w_gate[slab])
        wait_all(ups[slab])
        up = dot_nt(acts[...], w_up[slab])
        if slab == 0:
            wait_all(dy_in)
        wait_all(downs[slab])
        d_hidden = dot_nt(acts_dy[...], w_down[slab])
        sigmoid = 1.0 / (1.0 + jnp.exp(-gate))
        silu = gate * sigmoid
        hidden_ref[slab] = (silu * up).astype(bf16)
        d_gate_ref[slab] = (d_hidden * up * sigmoid * (1.0 + gate * (1.0 - sigmoid))).astype(bf16)
        d_up_ref[slab] = (d_hidden * silu).astype(bf16)
    for column in range(0, 2048, 512):
        here = slice(column, column + 512)
        part = dot_nn(d_gate_ref[0], w_gate[0, :, here]) + dot_nn(d_up_ref[0], w_up[0, :, here])
        part += dot_nn(d_gate_ref[1], w_gate[1, :, here]) + dot_nn(d_up_ref[1], w_up[1, :, here])
        part_ref[:, :, here] = part.astype(bf16).reshape(4, 128, 512)


def mlp(rows, dy_rows, weights):
    return kernel_call(
        mlp_kernel,
        (shape_of(2, 512, 688),) * 3 + (shape_of(4, 128, 2048),),
        (*rows, *dy_rows, *weights),
        [ROWS, ROWS]
        + [weight_scratch(688)] * 3,
        10 + 128,
        28,
        "mlp",
    )


def down_kernel(hidden_ref, *refs):
    weights, (part_ref, hidden, weight, sems) = refs[:20], refs[20:]
    load = Loader(sems)
    hidden_in = load.copy(hidden_ref, hidden)
    arrived = load.mlp_weight(weights, "down", weight)
    hidden_in.wait()
    wait_all(arrived[0] + arrived[1])
    part = dot_nn(hidden[0], weight[0]) + dot_nn(hidden[1], weight[1])
    part_ref[...] = part.astype(bf16).reshape(4, 128, 2048)


def project_down(hidden, weights):
    return kernel_call(
        down_kernel,
        shape_of(4, 128, 2048),
        (hidden, *weights),
        [pltpu.VMEM((2, 512, 688), bf16), weight_scratch(688)],
        1 + 32,
        8,
        "project_down",
    )


def feature_grads(acts, rows, store):
    for slab in range(2):
        for quarter in range(4):
            value = dot_tn(acts[slab], rows[:, quarter * 512 : (quarter + 1) * 512])
            core, turn = divmod(quarter, 2)
            for z in range(4):
                block = value[:, z * 128 : (z + 1) * 128].astype(bf16)
                store(core, slab * 8 + turn * 4 + z, block)


def mlp_grad_kernel(d_gate_ref, d_up_ref, hidden_ref, *refs):
    rows, dy_rows, outs = refs[:5], refs[5:9], (refs[9:11], refs[11:13])
    acts, acts_dy, hidden, sems = refs[13:]
    load = Loader(sems)
    acts_in = load.rows(rows, acts)
    hidden_in = [
        load.copy(ref, hidden.at[n]) for n, ref in enumerate((d_gate_ref, d_up_ref, hidden_ref))
    ]
    dy_in = load.rows(dy_rows, acts_dy)
    wait_all(acts_in)
    for n, name in enumerate(("gate", "up", "down")):
        hidden_in[n].wait()
        if n == 2:
            wait_all(dy_in)

        def store(core, k, block, name=name):
            y, z = ((k >> 2) & 1) * 2 + (k >> 3), k & 3
            for group, first_row, rows, at in MLP_ROWS[name]:
                place = outs[group][core].at[(y, z) if group == 0 else (z, y)]
                place[first_row : first_row + rows] = block[at : at + rows]

        feature_grads(hidden.at[n], acts if n < 2 else acts_dy, store)


def mlp_grad(d_gate, d_up, hidden, rows, dy_rows):
    return kernel_call(
        mlp_grad_kernel,
        (shape_of(4, 4, GROUP_A, 128),) * 2 + (shape_of(4, 4, GROUP_B, 128),) * 2,
        (d_gate, d_up, hidden, *rows, *dy_rows),
        [ROWS, ROWS, pltpu.VMEM((3, 2, 512, 688), bf16)],
        13,
        18,
        "mlp_grad",
    )


def out_back_kernel(source_ref, *refs):
    rows, weights = refs[:5], refs[5:7]
    out_ref, acts, weight, sems = refs[7:]
    load = Loader(sems, source_ref)
    acts_in = load.rows(rows, acts)
    arrived = load.weight(weights, 768, weight)
    wait_all(acts_in)
    for slab in range(2):
        wait_all(arrived[slab])
        value = dot_nt(acts[...], weight[slab]).astype(bf16)
        for j in range(4):
            for head in range(2):
                out_ref[j * 4 + slab * 2 + head] = value[
                    j * 128 : (j + 1) * 128, head * 128 : (head + 1) * 128
                ]


def out_back(source, rows, weights):
    return kernel_call(
        out_back_kernel,
        shape_of(16, 128, 128),
        (source, *rows, *weights),
        [ROWS, weight_scratch(256)],
        5 + 32,
        6,
        "out_back",
        smem=1,
    )


def unpack_heads(source, target):
    for p in range(16):
        j, slab, head = p >> 2, (p >> 1) & 1, p & 1
        for kind in range(3):
            column = (kind * 2 + head) * 128
            target[slab, j * 128 : (j + 1) * 128, column : column + 128] = source[p, kind]


def qkv_back_kernel(source_ref, dqkv_ref, mine_ref, theirs_ref, *refs):
    part_ref, dqkv, acts, weight, acc, sems = refs
    load = Loader(sems, source_ref)
    dqkv_in = load.copy(dqkv_ref, dqkv)
    arrived = load.weight((mine_ref, theirs_ref), 0, weight)
    dqkv_in.wait()
    unpack_heads(dqkv, acts)
    for slab in range(2):
        wait_all(arrived[slab])
        part = dot_nn(acts[slab], weight[slab])
        if slab == 0:
            acc[...] = part
        else:
            part_ref[...] = (acc[...] + part).astype(bf16).reshape(4, 128, 2048)


def qkv_back(source, dqkv, weights):
    return kernel_call(
        qkv_back_kernel,
        shape_of(4, 128, 2048),
        (source, dqkv, *weights),
        [
            pltpu.VMEM((16, 3, 128, 128), bf16),
            pltpu.VMEM((2, 512, 768), bf16),
            weight_scratch(768),
            pltpu.VMEM((512, 2048), f32),
        ],
        1 + 32,
        9,
        "qkv_back",
        smem=1,
    )


def qkv_grad_kernel(dqkv_ref, low_ref, *refs):
    rows1, rows3, outs = refs[:5], refs[5:10], refs[10:12]
    dqkv, low, acts, low_acts, in1, in3, sems = refs[12:]
    load = Loader(sems)
    low_in = load.copy(low_ref, low)
    in3_in = load.rows(rows3, in3)
    dqkv_in = load.copy(dqkv_ref, dqkv)
    in1_in = load.rows(rows1, in1)
    low_in.wait()
    for p in range(16):
        j, slab, head = p >> 2, (p >> 1) & 1, p & 1
        low_acts[slab, j * 128 : (j + 1) * 128, head * 128 : (head + 1) * 128] = low[p]
    wait_all(in3_in)

    def store_at(first):
        def store(core, k, block):
            y = ((k >> 2) & 1) * 2 + (k >> 3)
            outs[core][k & 3, y, first : first + block.shape[0]] = block

        return store

    feature_grads(low_acts, in3, store_at(768))
    dqkv_in.wait()
    unpack_heads(dqkv, acts)
    wait_all(in1_in)
    feature_grads(acts, in1, store_at(0))


def qkv_grad(dqkv, low, rows1, rows3):
    return kernel_call(
        qkv_grad_kernel,
        (shape_of(4, 4, 1024, 128),) * 2,
        (dqkv, low, *rows1, *rows3),
        [
            pltpu.VMEM((16, 3, 128, 128), bf16),
            pltpu.VMEM((16, 128, 128), bf16),
            pltpu.VMEM((2, 512, 768), bf16),
            pltpu.VMEM((2, 512, 256), bf16),
            ROWS,
            ROWS,
        ],
        12,
        10,
        "qkv_grad",
    )


def visible_end(ends_ref, first):
    places = first + lax.broadcasted_iota(jnp.int32, (1, TILE), 1)
    end = jnp.full((1, TILE), SEQ, jnp.int32)
    for j in range(10, -1, -1):
        end = jnp.where(places < ends_ref[j], ends_ref[j], end)
    return end


def key_blocks(i):
    return min(i + 2, SEQ // TILE)


def rows_of(ref, kind, i):
    return ref[2 * i : 2 * i + 2, kind].reshape(TILE, HEAD_DIM)


def masked(scores, end, kb):
    places = kb * TILE + lax.broadcasted_iota(jnp.int32, (TILE, TILE), 0)
    return jnp.where(places < end, scores, masked_score)


def attend_kernel(ends_ref, qkv_ref, low_ref, out_ref, lse_ref, score_ref, value_ref):
    for i in range(SEQ // TILE):
        value_ref[:, i * TILE : (i + 1) * TILE] = rows_of(qkv_ref, 2, i).astype(f32).T.astype(bf16)
    for i in range(SEQ // TILE):
        query = rows_of(qkv_ref, 0, i)
        end = visible_end(ends_ref, i * TILE)
        top = jnp.full((8, TILE), masked_score, f32)
        for kb in range(key_blocks(i)):
            scores = dot_nt(rows_of(qkv_ref, 1, kb), query) * (score_scale * log2_e)
            if kb >= i:
                scores = masked(scores, end, kb)
            score_ref[kb * TILE : (kb + 1) * TILE, :] = scores
            top = jnp.maximum(top, jnp.max(scores.reshape(TILE // 8, 8, TILE), axis=0))
        top = jnp.max(top, axis=0, keepdims=True)
        total = jnp.zeros((8, TILE), f32)
        acc = jnp.zeros((HEAD_DIM, TILE), f32)
        for kb in range(key_blocks(i)):
            weights = jnp.exp2(score_ref[kb * TILE : (kb + 1) * TILE, :] - top)
            total = total + jnp.sum(weights.reshape(TILE // 8, 8, TILE), axis=0)
            acc = acc + dot_nn(value_ref[:, kb * TILE : (kb + 1) * TILE], weights.astype(bf16))
        total = jnp.sum(total, axis=0, keepdims=True)
        attended = (acc / total).T
        out_ref[i * TILE : (i + 1) * TILE, :] = attended
        low_ref[2 * i : 2 * i + 2] = attended.astype(bf16).reshape(2, 128, HEAD_DIM)
        lse_ref[:, i * TILE : (i + 1) * TILE] = top + jnp.log2(total)


def attend(ends, qkv):
    return pl.pallas_call(
        attend_kernel,
        out_shape=(
            jax.ShapeDtypeStruct((16, 128, HEAD_DIM), bf16),
            jax.ShapeDtypeStruct((SEQ, HEAD_DIM), f32),
            jax.ShapeDtypeStruct((1, SEQ), f32),
        ),
        in_specs=[smem_spec(), vmem_spec()],
        out_specs=(vmem_spec(),) * 3,
        scratch_shapes=[pltpu.VMEM((SEQ, TILE), f32), pltpu.VMEM((HEAD_DIM, SEQ), bf16)],
        compiler_params=params(),
        cost_estimate=cost(8),
        name="attend",
    )(ends, qkv)


def attend_back_kernel(
    ends_ref, qkv_ref, grad_ref, out_ref, lse_ref, cos_ref, sin_ref, dqkv_ref, dk_ref, dv_ref
):
    dk_ref[...] = jnp.zeros_like(dk_ref)
    dv_ref[...] = jnp.zeros_like(dv_ref)

    def turn_back(gradient, i):
        here = slice(i * TILE, (i + 1) * TILE)
        gradient = gradient * score_scale
        turned = gradient * cos_ref[here, :] - pltpu.roll(gradient, 64, 1) * sin_ref[here, :]
        return turned.astype(bf16).reshape(2, 128, HEAD_DIM)

    for i in range(SEQ // TILE):
        here = slice(i * TILE, (i + 1) * TILE)
        query = rows_of(qkv_ref, 0, i)
        grad = grad_ref[2 * i : 2 * i + 2].reshape(TILE, HEAD_DIM)
        product = jnp.sum(grad.astype(f32) * out_ref[here, :], axis=1, keepdims=True)
        delta = jnp.broadcast_to(product, (TILE, 128)).T[0:1, :]
        lse = lse_ref[:, here]
        end = visible_end(ends_ref, i * TILE)
        dq = jnp.zeros((TILE, HEAD_DIM), f32)
        for kb in range(key_blocks(i)):
            there = slice(kb * TILE, (kb + 1) * TILE)
            key = rows_of(qkv_ref, 1, kb)
            scores = dot_nt(key, query) * (score_scale * log2_e)
            if kb >= i:
                scores = masked(scores, end, kb)
            probs = jnp.exp2(scores - lse)
            dv_ref[there, :] += dot_nn(probs.astype(bf16), grad)
            dprobs = dot_nt(rows_of(qkv_ref, 2, kb), grad)
            dscores = (probs * (dprobs - delta)).astype(bf16)
            dk_ref[there, :] += dot_nn(dscores, query)
            dq = dq + dot_tn(dscores, key)
        dqkv_ref[2 * i : 2 * i + 2, 0] = turn_back(dq, i)
    for i in range(SEQ // TILE):
        here = slice(i * TILE, (i + 1) * TILE)
        dqkv_ref[2 * i : 2 * i + 2, 1] = turn_back(dk_ref[here, :], i)
        dqkv_ref[2 * i : 2 * i + 2, 2] = dv_ref[here, :].astype(bf16).reshape(2, 128, HEAD_DIM)


def attend_back(ends, qkv, grad, out, lse, cosine, sine):
    return pl.pallas_call(
        attend_back_kernel,
        out_shape=jax.ShapeDtypeStruct((16, 3, 128, HEAD_DIM), bf16),
        in_specs=[smem_spec()] + [vmem_spec()] * 6,
        out_specs=vmem_spec(),
        scratch_shapes=[pltpu.VMEM((SEQ, HEAD_DIM), f32), pltpu.VMEM((SEQ, HEAD_DIM), f32)],
        compiler_params=params(),
        cost_estimate=cost(15),
        name="attend_back",
    )(ends, qkv, grad, out, lse, cosine, sine)


PLANE = ("yl", "yh", "z")


def plane_exchange(value):
    return lax.all_to_all(value, PLANE, split_axis=0, concat_axis=0, tiled=True)


def rotary(count):
    places = jnp.arange(count, dtype=jnp.int32).astype(f32)
    within = jnp.arange(HEAD_DIM, dtype=jnp.int32) % (HEAD_DIM // 2)
    inverse_freq = 10000.0 ** (within.astype(f32) * (-2.0 / HEAD_DIM))
    angles = places[:, None] * inverse_freq[None, :]
    sign = jnp.where(jnp.arange(HEAD_DIM) < HEAD_DIM // 2, -1.0, 1.0).astype(f32)
    return jnp.cos(angles), jnp.sin(angles) * sign


def inverse_rms(values):
    return lax.rsqrt(jnp.mean(values * values, axis=-1, keepdims=True) + norm_eps)


def norm_back(grad_normed, values, inverse, gain):
    scaled = grad_normed * gain
    gain_part = jnp.sum(grad_normed * values * inverse, axis=0)
    inner = jnp.mean(scaled * values, axis=-1, keepdims=True)
    return inverse * scaled - values * inverse**3 * inner, gain_part


def on_device(
    tokens,
    block_lengths,
    attn_gain,
    query_weight,
    key_weight,
    value_weight,
    out_weight,
    mlp_gain,
    gate_weight,
    up_weight,
    down_weight,
    output_grad,
):
    x, yl, yh, z, c = (lax.axis_index(name) for name in ("x", "yl", "yh", "z", "c"))
    blk = (yh * 4 + z) * 2 + c
    rel = jnp.arange(16, dtype=jnp.int32)
    place = ((yh ^ ((rel >> 2) & 1)) * 4 + (z ^ (rel & 3))) * 2 + (c ^ (rel >> 3))
    chosen = place[:, None] == rel[None, :]

    def relative(gain):
        return jnp.sum(jnp.where(chosen[:, :, None], gain.reshape(1, 16, 128), 0.0), axis=1)

    def absolute(gain):
        return jnp.sum(jnp.where(chosen[:, :, None], gain.reshape(16, 1, 128), 0.0), axis=0)

    first_gain = relative(attn_gain).reshape(1, 2048)
    second_gain = relative(mlp_gain).reshape(1, 2048)
    cosine, sine = rotary(SEQ)
    own_cosine = lax.dynamic_slice_in_dim(cosine, blk * 128, 128, 0)
    own_sine = lax.dynamic_slice_in_dim(sine, blk * 128, 128, 0)
    sequence = (x ^ (blk >> 2)) * 2 + yl
    ends = jnp.cumsum(lax.dynamic_slice_in_dim(block_lengths, sequence, 1, 0)[0])

    normed1, tok, dy = prepare(place, tokens[0], output_grad[0], first_gain)
    tok = tok.astype(f32)
    blkaxes = ("yh", "z", "c")

    def exchange(value):
        return lax.all_to_all(value, blkaxes, split_axis=0, concat_axis=0, tiled=True)

    shard_a = jnp.concatenate([gate_weight.T, up_weight.T[:336]], axis=0)
    shard_b = jnp.concatenate([up_weight.T[336:], down_weight], axis=0)
    source = ((yl ^ (rel >> 3)) * 2 + (yh ^ ((rel >> 2) & 1))) * 4 + (z ^ (rel & 3))

    rows1 = gather4(normed1, "x")
    dy_rows = spread4(after(dy, rows1[4]), "x")
    mine = plane_exchange(share(query_weight, key_weight, value_weight, out_weight))
    mine = after(mine, *rows1[2:4], *dy_rows[1:], cosine, sine)
    w_attn = (mine, swap(mine, "c", 1))

    orders = "zy", "yz"
    shards = after(shard_a, mine), after(shard_b, mine)
    pieces = [spread4(v, o[0]) for v, o in zip(shards, orders)]
    qkv = project_qkv(source, rows1, w_attn, own_cosine, own_sine)
    qkv = exchange(after(qkv, *pieces[0], *pieces[1]))
    plane = [stacked(v) for v in pieces]
    low, attended, lse = attend(ends, after(qkv, *plane))
    low = exchange(low)
    near = [[swap(v, o[1], 1), swap(v, o[1], 3)] for v, o in zip(plane, orders)]
    part = project_out(source, after(low, *near[0], *near[1]), w_attn)
    residual = tok + scatter4([[part[k]] for k in range(4)], "x")
    groups = [gather_far(v, n, o[1]) for v, n, o in zip(plane, near, orders)]
    w_mlp = []
    for group in groups:
        held = [after(piece, residual) for piece in group]
        w_mlp += [*group, *(swap(piece, "c", 1) for piece in held)]
    inverse2 = inverse_rms(residual)
    normed2 = (residual * inverse2 * second_gain).astype(bf16)
    rows2 = gather4(normed2, "x")
    hidden, d_gate, d_up, part = mlp(rows2, dy_rows, w_mlp)

    far = scatter_far([part[2]], "x")
    near1, near3 = scatter_near([part[1]], [part[3]], far, "x")
    grads = mlp_grad(after(d_gate, *far), d_up, hidden, rows2, dy_rows)
    d_normed2 = add(part[0], after(near1, grads[0]), near3)
    back2, second_part = norm_back(d_normed2, residual, inverse2, second_gain)
    d_residual = dy.astype(f32) + back2
    d_attn = d_residual.astype(bf16)
    rows3 = gather4(d_attn, "x")

    orders = "yz", "zy"
    mine = grads[0], grads[2]
    got = [swap(after(v, d_attn), "c", 1) for v in (grads[1], grads[3])]
    terms = [pairs(m, g) for m, g in zip(mine, got)]
    sums = [far_sums(t[2]) for t in terms]
    rows3 = (after(rows3[0], *sums[0], *sums[1]),) + rows3[1:]
    far = [(swap(v[0], o[0], 1), swap(v[1], o[0], 3)) for v, o in zip(sums, orders)]
    d_out = out_back(source, rows3, w_attn)
    terms = [pairs(after(m, d_out), g) for m, g in zip(mine, got)]
    sums = [near_sums(t[1], t[3], f) for t, f in zip(terms, far)]
    d_out = exchange(d_out)
    d_out = after(d_out, *sums[0], *sums[1])
    near = [(swap(v[0], o[0], 1), swap(v[1], o[0], 3)) for v, o in zip(sums, orders)]
    dqkv = attend_back(ends, qkv, d_out, attended, lse, cosine, sine)
    dqkv = after(dqkv, *near[0], *near[1])
    down_part = project_down(after(hidden, dqkv), w_mlp)
    out_far = scatter_far([down_part[2]], "x")
    mine = after(mine[0], down_part), after(mine[1], down_part)
    terms = [pairs(m, g) for m, g in zip(mine, got)]
    along = [add(*t[0], *n).astype(bf16) for t, n in zip(terms, near)]
    dqkv = after(exchange(dqkv), *out_far, *along)

    qkv_mine, qkv_theirs = qkv_grad(dqkv, low, rows1, rows3)
    qkv_got = swap(qkv_theirs, "c", 1)
    part = qkv_back(source, after(dqkv, qkv_mine), w_attn)
    sums = far_sums(pairs(qkv_mine, qkv_got)[2])
    qkv_far = swap(sums[0], "z", 1), swap(sums[1], "z", 3)
    part = after(part, *sums)
    far = scatter_far([part[2]], "x")
    qkv_terms = pairs(after(qkv_mine, *far), qkv_got)
    sums = near_sums(qkv_terms[1], qkv_terms[3], qkv_far)
    qkv_near = swap(sums[0], "z", 1), swap(sums[1], "z", 3)
    d_near = scatter_near([part[1]], [part[3]], far, "x")
    d_normed1 = add(part[0], *d_near)
    out_near = scatter_near([after(down_part[1], *d_near)], [down_part[3]], out_far, "x")
    output = residual + add(down_part[0], *out_near)
    layer_output = restore(place, output.astype(bf16))[None]
    back1, first_part = norm_back(d_normed1, tok, inverse_rms(tok), first_gain)
    input_grad = d_residual + back1
    along = [after(v, *sums) for v in along]
    grad_a, grad_b = (
        collect4([[v[k]] for k in range(4)], o[1]) for v, o in zip(along, orders)
    )
    along = add(*qkv_terms[0], *qkv_near).astype(bf16)
    grad_qkv = collect4([[along[k]] for k in range(4)], "y")

    gains = jnp.concatenate([absolute(first_part), absolute(second_part)], axis=0)
    gains = total4(total4(gains, "x"), "y")
    gains = total4(after(gains, *qkv_near), "z")
    gains = gains + swap(gains, "c", 1)
    input_grad = restore(place, input_grad)[None]
    return (
        layer_output,
        input_grad,
        gains[:16].reshape(2048),
        grad_qkv[:256].T,
        grad_qkv[256:512].T,
        grad_qkv[512:768].T,
        grad_qkv[768:],
        gains[16:].reshape(2048),
        grad_a[:688].T,
        jnp.concatenate([grad_a[688:], grad_b[:352]], axis=0).T,
        grad_b[352:],
    )


def solution(mesh):
    fine = Mesh(mesh.devices.reshape(4, 2, 2, 4, 2), ("x", "yl", "yh", "z", "c"))
    head, blk = ("x", "yl"), ("yh", "z", "c")
    rows = P(head, blk, None)
    wide, tall = P(blk, head), P(head, blk)
    return jax.shard_map(
        on_device,
        mesh=fine,
        in_specs=(rows, P(), P(), wide, wide, wide, tall, P(), wide, wide, tall, rows),
        out_specs=(rows, rows, P(), wide, wide, wide, tall, P(), wide, wide, tall),
        check_vma=False,
    )
```

```python
import functools

import jax
import jax.numpy as jnp
from jax import lax
from jax.experimental import pallas as pl
from jax.experimental.pallas import tpu as pltpu
from jax.sharding import Mesh
from jax.sharding import PartitionSpec as P

HEAD_DIM = 128
SEQ = 2048
TILE = 256
norm_eps = 1e-05
masked_score = -1e30
score_scale = HEAD_DIM ** (-0.5)
log2_e = 1.4426950408889634
f32 = jnp.float32
bf16 = jnp.bfloat16
VMEM_LIMIT = 56 * 1024 * 1024

Y_STEP = {1: 2, 2: 1, 3: 3}


def swap(value, axis, step):
    if axis == "y":
        names, count, step = ("yl", "yh"), 4, Y_STEP[step]
    else:
        names, count = axis, lax.axis_size(axis)
    return lax.ppermute(value, names, [(i, i ^ step) for i in range(count)])


def middle(rows):
    return (rows // 2 + 15) // 16 * 16


def gather4(value, axis, hold=()):
    near = swap(value, axis, 1), swap(value, axis, 3)
    return gather_far(value, near, axis, hold)


def gather_far(value, near, axis, hold=()):
    half = middle(value.shape[0]) if value.ndim == 2 else value.shape[0] // 2
    near1, near3 = near
    far1 = swap(after(near3[:half], *hold), axis, 1)
    return value, near1, far1, swap(near1[half:], axis, 3), near3


def spread4(value, axis):
    return (value, *(swap(value, axis, step) for step in (1, 2, 3)))


def collect4(parts, axis, earlier=()):
    own = parts[0]
    sums = [add(*terms).astype(bf16) for terms in parts[1:]]
    return add(*own, *(swap(after(v, *earlier), axis, k + 1) for k, v in enumerate(sums)))


def add(*values):
    return functools.reduce(lambda a, b: a + b, [value.astype(f32) for value in values])


def after(value, *earlier):
    return lax.optimization_barrier((value, *earlier))[0] if earlier else value


def far_sums(part2):
    rows = part2[0].shape[0]
    half = middle(rows) if part2[0].ndim == 2 else rows // 2
    return (
        add(*[term[:half] for term in part2]).astype(bf16),
        add(*[term[half:] for term in part2]).astype(bf16),
    )


def scatter_far(part2, axis):
    far_a, far_b = far_sums(part2)
    return swap(far_a, axis, 1), swap(far_b, axis, 3)


def near_sums(part1, part3, far):
    from1, from3 = far
    half = from1.shape[0]
    part1 = jnp.concatenate(
        [
            add(*[term[:half] for term in part1]).astype(bf16),
            add(from3, *[term[half:] for term in part1]).astype(bf16),
        ],
        axis=0,
    )
    part3 = jnp.concatenate(
        [
            add(from1, *[term[:half] for term in part3]).astype(bf16),
            add(*[term[half:] for term in part3]).astype(bf16),
        ],
        axis=0,
    )
    return part1, part3


def scatter_near(part1, part3, far, axis, hold=()):
    part1, part3 = near_sums(part1, part3, far)
    return swap(after(part1, *hold), axis, 1), swap(part3, axis, 3)


def scatter4(parts, axis):
    own, part1, part2, part3 = parts
    return add(*scatter_near(part1, part3, scatter_far(part2, axis), axis), *own)


def pairs(mine, got):
    return [[mine[k], got[k]] for k in range(4)]


def total4(value, axis):
    return (value + swap(value, axis, 1)) + (swap(value, axis, 2) + swap(value, axis, 3))


def vmem_spec():
    return pl.BlockSpec(memory_space=pltpu.VMEM)


def smem_spec():
    return pl.BlockSpec(memory_space=pltpu.SMEM)


def params():
    return pltpu.CompilerParams(vmem_limit_bytes=VMEM_LIMIT)


def block_at(place_ref, index):
    return pl.ds(pl.multiple_of(place_ref[index] * 128, 128), 128)


def prepare_kernel(place_ref, tok_ref, dy_ref, gain_ref, h1_ref, tok_out, dy_out):
    total = jnp.zeros((128, 128), f32)
    for r in range(16):
        part = tok_ref[:, r * 128 : (r + 1) * 128].astype(f32)
        total = total + part * part
    inverse = lax.rsqrt(jnp.sum(total, axis=1, keepdims=True) / 2048.0 + norm_eps)
    for r in range(16):
        here = slice(r * 128, (r + 1) * 128)
        there = block_at(place_ref, r)
        part = tok_ref[:, there]
        tok_out[:, here] = part
        dy_out[:, here] = dy_ref[:, there]
        h1_ref[:, here] = (part.astype(f32) * inverse * gain_ref[:, here]).astype(bf16)


def prepare(place, tok, dy, gain):
    out = jax.ShapeDtypeStruct((128, 2048), bf16)
    return pl.pallas_call(
        prepare_kernel,
        out_shape=(out, out, out),
        in_specs=[smem_spec(), vmem_spec(), vmem_spec(), vmem_spec()],
        out_specs=(vmem_spec(),) * 3,
        compiler_params=params(),
        cost_estimate=cost(2.5),
        name="prepare",
    )(place, tok, dy, gain)


def share_kernel(query_ref, key_ref, value_ref, out_w_ref, copies_ref, rows, sems):
    for n, ref in enumerate((query_ref, key_ref, value_ref)):
        rows[n * 256 : (n + 1) * 256] = ref[...].astype(f32).T.astype(bf16)
    rows[768:] = out_w_ref[...]
    made = [pltpu.make_async_copy(rows, copies_ref.at[k], sems.at[k]) for k in range(16)]
    for copy in made:
        copy.start()
    for copy in made:
        copy.wait()


def share(query, key, value, out_weight):
    return pl.pallas_call(
        share_kernel,
        out_shape=jax.ShapeDtypeStruct((16, 1024, 128), bf16),
        in_specs=[vmem_spec()] * 4,
        out_specs=pl.BlockSpec(memory_space=pl.ANY),
        scratch_shapes=[pltpu.VMEM((1024, 128), bf16), pltpu.SemaphoreType.DMA((16,))],
        compiler_params=params(),
        cost_estimate=cost(3),
        name="share",
    )(query, key, value, out_weight)


def restore_kernel(place_ref, in_ref, out_ref):
    for r in range(16):
        out_ref[:, block_at(place_ref, r)] = in_ref[:, r * 128 : (r + 1) * 128]


def restore(place, value):
    return pl.pallas_call(
        restore_kernel,
        out_shape=jax.ShapeDtypeStruct(value.shape, value.dtype),
        in_specs=[smem_spec(), vmem_spec()],
        out_specs=vmem_spec(),
        compiler_params=params(),
        cost_estimate=cost(2),
        name="restore",
    )(place, value)


def dot_nt(left, right):
    return lax.dot_general(left, right, (((1,), (1,)), ((), ())), preferred_element_type=f32)


def dot_nn(left, right):
    return lax.dot_general(left, right, (((1,), (0,)), ((), ())), preferred_element_type=f32)


def dot_tn(left, right):
    return lax.dot_general(left, right, (((0,), (0,)), ((), ())), preferred_element_type=f32)


def any_spec():
    return pl.BlockSpec(memory_space=pl.ANY)


def pieces_of(order):
    found = []
    for core in range(2):
        for second in range(4):
            for first in range(4):
                z, y = (first, second) if order == "zy" else (second, first)
                slab, turn = y & 1, y >> 1
                if second == 2:
                    array, entry = (2, first) if first < 2 else (3, first - 2)
                else:
                    array, entry = {0: 0, 1: 1, 3: 4}[second], first
                found.append((core * 5 + array, entry, slab, core * 8 + turn * 4 + z))
    return found


GROUP_A, GROUP_B = 1024, 1040
MLP_ROWS = {
    "gate": ((0, 0, 688, 0),),
    "up": ((0, 688, 336, 0), (1, 0, 352, 336)),
    "down": ((1, 352, 688, 0),),
}


class Loader:
    def __init__(self, sems, source_ref=None):
        self.sems = sems
        self.source_ref = source_ref
        self.used = 0

    def copy(self, source, target):
        made = pltpu.make_async_copy(source, target, self.sems.at[self.used])
        self.used += 1
        made.start()
        return made

    def weight(self, refs, first_row, target, source_ref=None):
        source_ref = self.source_ref if source_ref is None else source_ref
        waits = ([], [])
        rows = target.shape[1]
        for slab in range(2):
            for core in range(2):
                for k in range(8):
                    block = core * 8 + k
                    waits[slab].append(
                        self.copy(
                            refs[core].at[source_ref[slab * 8 + k], first_row : first_row + rows],
                            target.at[slab, :, block * 128 : (block + 1) * 128],
                        )
                    )
        return waits

    def mlp_weight(self, pieces, name, target, slabs=(0, 1)):
        waits = ([], [])
        for group, first_row, rows, at in MLP_ROWS[name]:
            refs = pieces[group * 10 : group * 10 + 10]
            for array, entry, slab, block in pieces_of(("zy", "yz")[group]):
                if slab not in slabs:
                    continue
                waits[slab].append(
                    self.copy(
                        refs[array].at[entry, first_row : first_row + rows],
                        target.at[slab, at : at + rows, block * 128 : (block + 1) * 128],
                    )
                )
        return waits

    def rows(self, refs, target):
        copies, first = [], 0
        for ref in refs:
            copies.append(self.copy(ref, target.at[first : first + ref.shape[0]]))
            first += ref.shape[0]
        return copies


def wait_all(copies):
    for made in copies:
        made.wait()


def cost(micros):
    return pl.CostEstimate(flops=int(micros * 1.15e9), bytes_accessed=0, transcendentals=0)


def kernel_call(kernel, out_shape, args, scratch, copies, micros, name, smem=0):
    specs = [any_spec()] * (len(args) - smem)
    return pl.pallas_call(
        kernel,
        out_shape=out_shape,
        in_specs=[smem_spec()] * smem + specs,
        out_specs=jax.tree.map(lambda _: vmem_spec(), out_shape),
        scratch_shapes=list(scratch) + [pltpu.SemaphoreType.DMA((copies,))],
        compiler_params=params(),
        cost_estimate=cost(micros),
        name=name,
    )(*args)


def shape_of(*dims, dtype=bf16):
    return jax.ShapeDtypeStruct(dims, dtype)


ROWS = pltpu.VMEM((512, 2048), bf16)


def weight_scratch(rows):
    return pltpu.VMEM((2, rows, 2048), bf16)


def stack_kernel(own, near1, far, near3, out_ref, sems):
    load = Loader(sems)
    wait_all([load.copy(ref, out_ref.at[n]) for n, ref in enumerate((own, near1, far, near3))])


def stacked(parts):
    own = parts[0]
    return pl.pallas_call(
        stack_kernel,
        out_shape=shape_of(4, *own.shape),
        in_specs=[any_spec()] * 4,
        out_specs=vmem_spec(),
        scratch_shapes=[pltpu.SemaphoreType.DMA((4,))],
        compiler_params=params(),
        cost_estimate=cost(2.5),
        name="stack",
    )(*parts)


def qkv_kernel(source_ref, *refs):
    rows, weights = refs[:5], refs[5:7]
    cos_ref, sin_ref, out_ref, acts, weight, tables, sems = refs[7:]
    load = Loader(sems, source_ref)
    small = [load.copy(cos_ref, tables.at[0]), load.copy(sin_ref, tables.at[1])]
    acts_in = load.rows(rows, acts)
    arrived = load.weight(weights, 0, weight)
    wait_all(small + acts_in)
    for slab in range(2):
        wait_all(arrived[slab])
        for kind in range(3):
            pre = dot_nt(acts[...], weight[slab, kind * 256 : (kind + 1) * 256])
            for head in range(2):
                for j in range(4):
                    tile = pre[j * 128 : (j + 1) * 128, head * 128 : (head + 1) * 128]
                    if kind < 2:
                        tile = tile * tables[0] + pltpu.roll(tile, 64, 1) * tables[1]
                    out_ref[j * 4 + slab * 2 + head, kind] = tile.astype(bf16)


def project_qkv(source, rows, weights, cosine, sine):
    return kernel_call(
        qkv_kernel,
        shape_of(16, 3, 128, 128),
        (source, *rows, *weights, cosine, sine),
        [ROWS, weight_scratch(768), pltpu.VMEM((2, 128, 128), f32)],
        7 + 32,
        10,
        "project_qkv",
        smem=1,
    )


def out_kernel(source_ref, low_ref, mine_ref, theirs_ref, part_ref, low, acts, weight, sems):
    load = Loader(sems, source_ref)
    low_in = load.copy(low_ref, low)
    arrived = load.weight((mine_ref, theirs_ref), 768, weight)
    low_in.wait()
    for p in range(16):
        j, slab, head = p >> 2, (p >> 1) & 1, p & 1
        acts[slab, j * 128 : (j + 1) * 128, head * 128 : (head + 1) * 128] = low[p]
    wait_all(arrived[0] + arrived[1])
    for j in range(0, 4, 2):
        here = slice(j * 128, (j + 2) * 128)
        part = dot_nn(acts[0, here], weight[0]) + dot_nn(acts[1, here], weight[1])
        part_ref[j : j + 2] = part.astype(bf16).reshape(2, 128, 2048)


def project_out(source, low, weights):
    return kernel_call(
        out_kernel,
        shape_of(4, 128, 2048),
        (source, low, *weights),
        [
            pltpu.VMEM((16, 128, 128), bf16),
            pltpu.VMEM((2, 512, 256), bf16),
            weight_scratch(256),
        ],
        1 + 32,
        5,
        "project_out",
        smem=1,
    )


def mlp_kernel(*refs):
    rows, dy_rows, weights = refs[:5], refs[5:9], refs[9:29]
    hidden_ref, d_gate_ref, d_up_ref, part_ref = refs[29:33]
    acts, acts_dy, w_gate, w_up, w_down, sems = refs[33:]
    load = Loader(sems)
    acts_in = load.rows(rows, acts)
    names = ("gate", w_gate), ("up", w_up), ("down", w_down)
    first = [load.mlp_weight(weights, *name, slabs=(0,))[0] for name in names[:2]]
    dy_in = load.rows(dy_rows, acts_dy)
    first.append(load.mlp_weight(weights, *names[2], slabs=(0,))[0])
    second = [load.mlp_weight(weights, *name, slabs=(1,))[1] for name in names]
    gates, ups, downs = zip(first, second)
    wait_all(acts_in)
    for slab in range(2):
        wait_all(gates[slab])
        gate = dot_nt(acts[...], w_gate[slab])
        wait_all(ups[slab])
        up = dot_nt(acts[...], w_up[slab])
        if slab == 0:
            wait_all(dy_in)
        wait_all(downs[slab])
        d_hidden = dot_nt(acts_dy[...], w_down[slab])
        sigmoid = 1.0 / (1.0 + jnp.exp(-gate))
        silu = gate * sigmoid
        hidden_ref[slab] = (silu * up).astype(bf16)
        d_gate_ref[slab] = (d_hidden * up * sigmoid * (1.0 + gate * (1.0 - sigmoid))).astype(bf16)
        d_up_ref[slab] = (d_hidden * silu).astype(bf16)
    for column in range(0, 2048, 512):
        here = slice(column, column + 512)
        part = dot_nn(d_gate_ref[0], w_gate[0, :, here]) + dot_nn(d_up_ref[0], w_up[0, :, here])
        part += dot_nn(d_gate_ref[1], w_gate[1, :, here]) + dot_nn(d_up_ref[1], w_up[1, :, here])
        part_ref[:, :, here] = part.astype(bf16).reshape(4, 128, 512)


def mlp(rows, dy_rows, weights):
    return kernel_call(
        mlp_kernel,
        (shape_of(2, 512, 688),) * 3 + (shape_of(4, 128, 2048),),
        (*rows, *dy_rows, *weights),
        [ROWS, ROWS]
        + [weight_scratch(688)] * 3,
        10 + 128,
        28,
        "mlp",
    )


def down_kernel(hidden_ref, *refs):
    weights, (part_ref, hidden, weight, sems) = refs[:20], refs[20:]
    load = Loader(sems)
    hidden_in = load.copy(hidden_ref, hidden)
    arrived = load.mlp_weight(weights, "down", weight)
    hidden_in.wait()
    wait_all(arrived[0] + arrived[1])
    part = dot_nn(hidden[0], weight[0]) + dot_nn(hidden[1], weight[1])
    part_ref[...] = part.astype(bf16).reshape(4, 128, 2048)


def project_down(hidden, weights):
    return kernel_call(
        down_kernel,
        shape_of(4, 128, 2048),
        (hidden, *weights),
        [pltpu.VMEM((2, 512, 688), bf16), weight_scratch(688)],
        1 + 32,
        8,
        "project_down",
    )


def feature_grads(acts, rows, store):
    for slab in range(2):
        for quarter in range(4):
            value = dot_tn(acts[slab], rows[:, quarter * 512 : (quarter + 1) * 512])
            core, turn = divmod(quarter, 2)
            for z in range(4):
                block = value[:, z * 128 : (z + 1) * 128].astype(bf16)
                store(core, slab * 8 + turn * 4 + z, block)


def mlp_grad_kernel(d_gate_ref, d_up_ref, hidden_ref, *refs):
    rows, dy_rows, outs = refs[:5], refs[5:9], (refs[9:11], refs[11:13])
    acts, acts_dy, hidden, sems = refs[13:]
    load = Loader(sems)
    acts_in = load.rows(rows, acts)
    hidden_in = [
        load.copy(ref, hidden.at[n]) for n, ref in enumerate((d_gate_ref, d_up_ref, hidden_ref))
    ]
    dy_in = load.rows(dy_rows, acts_dy)
    wait_all(acts_in)
    for n, name in enumerate(("gate", "up", "down")):
        hidden_in[n].wait()
        if n == 2:
            wait_all(dy_in)

        def store(core, k, block, name=name):
            y, z = ((k >> 2) & 1) * 2 + (k >> 3), k & 3
            for group, first_row, rows, at in MLP_ROWS[name]:
                place = outs[group][core].at[(y, z) if group == 0 else (z, y)]
                place[first_row : first_row + rows] = block[at : at + rows]

        feature_grads(hidden.at[n], acts if n < 2 else acts_dy, store)


def mlp_grad(d_gate, d_up, hidden, rows, dy_rows):
    return kernel_call(
        mlp_grad_kernel,
        (shape_of(4, 4, GROUP_A, 128),) * 2 + (shape_of(4, 4, GROUP_B, 128),) * 2,
        (d_gate, d_up, hidden, *rows, *dy_rows),
        [ROWS, ROWS, pltpu.VMEM((3, 2, 512, 688), bf16)],
        13,
        18,
        "mlp_grad",
    )


def out_back_kernel(source_ref, *refs):
    rows, weights = refs[:5], refs[5:7]
    out_ref, acts, weight, sems = refs[7:]
    load = Loader(sems, source_ref)
    acts_in = load.rows(rows, acts)
    arrived = load.weight(weights, 768, weight)
    wait_all(acts_in)
    for slab in range(2):
        wait_all(arrived[slab])
        value = dot_nt(acts[...], weight[slab]).astype(bf16)
        for j in range(4):
            for head in range(2):
                out_ref[j * 4 + slab * 2 + head] = value[
                    j * 128 : (j + 1) * 128, head * 128 : (head + 1) * 128
                ]


def out_back(source, rows, weights):
    return kernel_call(
        out_back_kernel,
        shape_of(16, 128, 128),
        (source, *rows, *weights),
        [ROWS, weight_scratch(256)],
        5 + 32,
        6,
        "out_back",
        smem=1,
    )


def unpack_heads(source, target):
    for p in range(16):
        j, slab, head = p >> 2, (p >> 1) & 1, p & 1
        for kind in range(3):
            column = (kind * 2 + head) * 128
            target[slab, j * 128 : (j + 1) * 128, column : column + 128] = source[p, kind]


def qkv_back_kernel(source_ref, dqkv_ref, mine_ref, theirs_ref, *refs):
    part_ref, dqkv, acts, weight, acc, sems = refs
    load = Loader(sems, source_ref)
    dqkv_in = load.copy(dqkv_ref, dqkv)
    arrived = load.weight((mine_ref, theirs_ref), 0, weight)
    dqkv_in.wait()
    unpack_heads(dqkv, acts)
    for slab in range(2):
        wait_all(arrived[slab])
        part = dot_nn(acts[slab], weight[slab])
        if slab == 0:
            acc[...] = part
        else:
            part_ref[...] = (acc[...] + part).astype(bf16).reshape(4, 128, 2048)


def qkv_back(source, dqkv, weights):
    return kernel_call(
        qkv_back_kernel,
        shape_of(4, 128, 2048),
        (source, dqkv, *weights),
        [
            pltpu.VMEM((16, 3, 128, 128), bf16),
            pltpu.VMEM((2, 512, 768), bf16),
            weight_scratch(768),
            pltpu.VMEM((512, 2048), f32),
        ],
        1 + 32,
        9,
        "qkv_back",
        smem=1,
    )


def qkv_grad_kernel(dqkv_ref, low_ref, *refs):
    rows1, rows3, outs = refs[:5], refs[5:10], refs[10:12]
    dqkv, low, acts, low_acts, in1, in3, sems = refs[12:]
    load = Loader(sems)
    low_in = load.copy(low_ref, low)
    in3_in = load.rows(rows3, in3)
    dqkv_in = load.copy(dqkv_ref, dqkv)
    in1_in = load.rows(rows1, in1)
    low_in.wait()
    for p in range(16):
        j, slab, head = p >> 2, (p >> 1) & 1, p & 1
        low_acts[slab, j * 128 : (j + 1) * 128, head * 128 : (head + 1) * 128] = low[p]
    wait_all(in3_in)

    def store_at(first):
        def store(core, k, block):
            y = ((k >> 2) & 1) * 2 + (k >> 3)
            outs[core][k & 3, y, first : first + block.shape[0]] = block

        return store

    feature_grads(low_acts, in3, store_at(768))
    dqkv_in.wait()
    unpack_heads(dqkv, acts)
    wait_all(in1_in)
    feature_grads(acts, in1, store_at(0))


def qkv_grad(dqkv, low, rows1, rows3):
    return kernel_call(
        qkv_grad_kernel,
        (shape_of(4, 4, 1024, 128),) * 2,
        (dqkv, low, *rows1, *rows3),
        [
            pltpu.VMEM((16, 3, 128, 128), bf16),
            pltpu.VMEM((16, 128, 128), bf16),
            pltpu.VMEM((2, 512, 768), bf16),
            pltpu.VMEM((2, 512, 256), bf16),
            ROWS,
            ROWS,
        ],
        12,
        10,
        "qkv_grad",
    )


def visible_end(ends_ref, first):
    places = first + lax.broadcasted_iota(jnp.int32, (1, TILE), 1)
    end = jnp.full((1, TILE), SEQ, jnp.int32)
    for j in range(10, -1, -1):
        end = jnp.where(places < ends_ref[j], ends_ref[j], end)
    return end


def key_blocks(i):
    return min(i + 2, SEQ // TILE)


def rows_of(ref, kind, i):
    return ref[2 * i : 2 * i + 2, kind].reshape(TILE, HEAD_DIM)


def masked(scores, end, kb):
    places = kb * TILE + lax.broadcasted_iota(jnp.int32, (TILE, TILE), 0)
    return jnp.where(places < end, scores, masked_score)


def attend_kernel(ends_ref, qkv_ref, low_ref, out_ref, lse_ref, score_ref, value_ref):
    for i in range(SEQ // TILE):
        value_ref[:, i * TILE : (i + 1) * TILE] = rows_of(qkv_ref, 2, i).astype(f32).T.astype(bf16)
    for i in range(SEQ // TILE):
        query = rows_of(qkv_ref, 0, i)
        end = visible_end(ends_ref, i * TILE)
        top = jnp.full((8, TILE), masked_score, f32)
        for kb in range(key_blocks(i)):
            scores = dot_nt(rows_of(qkv_ref, 1, kb), query) * (score_scale * log2_e)
            if kb >= i:
                scores = masked(scores, end, kb)
            score_ref[kb * TILE : (kb + 1) * TILE, :] = scores
            top = jnp.maximum(top, jnp.max(scores.reshape(TILE // 8, 8, TILE), axis=0))
        top = jnp.max(top, axis=0, keepdims=True)
        total = jnp.zeros((8, TILE), f32)
        acc = jnp.zeros((HEAD_DIM, TILE), f32)
        for kb in range(key_blocks(i)):
            weights = jnp.exp2(score_ref[kb * TILE : (kb + 1) * TILE, :] - top)
            total = total + jnp.sum(weights.reshape(TILE // 8, 8, TILE), axis=0)
            acc = acc + dot_nn(value_ref[:, kb * TILE : (kb + 1) * TILE], weights.astype(bf16))
        total = jnp.sum(total, axis=0, keepdims=True)
        attended = (acc / total).T
        out_ref[i * TILE : (i + 1) * TILE, :] = attended
        low_ref[2 * i : 2 * i + 2] = attended.astype(bf16).reshape(2, 128, HEAD_DIM)
        lse_ref[:, i * TILE : (i + 1) * TILE] = top + jnp.log2(total)


def attend(ends, qkv):
    return pl.pallas_call(
        attend_kernel,
        out_shape=(
            jax.ShapeDtypeStruct((16, 128, HEAD_DIM), bf16),
            jax.ShapeDtypeStruct((SEQ, HEAD_DIM), f32),
            jax.ShapeDtypeStruct((1, SEQ), f32),
        ),
        in_specs=[smem_spec(), vmem_spec()],
        out_specs=(vmem_spec(),) * 3,
        scratch_shapes=[pltpu.VMEM((SEQ, TILE), f32), pltpu.VMEM((HEAD_DIM, SEQ), bf16)],
        compiler_params=params(),
        cost_estimate=cost(8),
        name="attend",
    )(ends, qkv)


def attend_back_kernel(
    ends_ref, qkv_ref, grad_ref, out_ref, lse_ref, cos_ref, sin_ref, dqkv_ref, dk_ref, dv_ref, key_ref
):
    for i in range(SEQ // TILE):
        key_ref[:, i * TILE : (i + 1) * TILE] = rows_of(qkv_ref, 1, i).astype(f32).T.astype(bf16)
    dk_ref[...] = jnp.zeros_like(dk_ref)
    dv_ref[...] = jnp.zeros_like(dv_ref)

    def turn_back(gradient, i):
        here = slice(i * TILE, (i + 1) * TILE)
        gradient = gradient * score_scale
        turned = gradient * cos_ref[here, :] - pltpu.roll(gradient, 64, 1) * sin_ref[here, :]
        return turned.astype(bf16).reshape(2, 128, HEAD_DIM)

    for i in range(SEQ // TILE):
        here = slice(i * TILE, (i + 1) * TILE)
        query = rows_of(qkv_ref, 0, i)
        grad = grad_ref[2 * i : 2 * i + 2].reshape(TILE, HEAD_DIM)
        product = jnp.sum(grad.astype(f32) * out_ref[here, :], axis=1, keepdims=True)
        delta = jnp.broadcast_to(product, (TILE, 128)).T[0:1, :]
        lse = lse_ref[:, here]
        end = visible_end(ends_ref, i * TILE)
        dq = jnp.zeros((HEAD_DIM, TILE), f32)
        for kb in range(key_blocks(i)):
            there = slice(kb * TILE, (kb + 1) * TILE)
            key = rows_of(qkv_ref, 1, kb)
            scores = dot_nt(key, query) * (score_scale * log2_e)
            if kb >= i:
                scores = masked(scores, end, kb)
            probs = jnp.exp2(scores - lse)
            dv_ref[there, :] += dot_nn(probs.astype(bf16), grad)
            dprobs = dot_nt(rows_of(qkv_ref, 2, kb), grad)
            dscores = (probs * (dprobs - delta)).astype(bf16)
            dk_ref[there, :] += dot_nn(dscores, query)
            dq = dq + dot_nn(key_ref[:, there], dscores)
        dqkv_ref[2 * i : 2 * i + 2, 0] = turn_back(dq.T, i)
    for i in range(SEQ // TILE):
        here = slice(i * TILE, (i + 1) * TILE)
        dqkv_ref[2 * i : 2 * i + 2, 1] = turn_back(dk_ref[here, :], i)
        dqkv_ref[2 * i : 2 * i + 2, 2] = dv_ref[here, :].astype(bf16).reshape(2, 128, HEAD_DIM)


def attend_back(ends, qkv, grad, out, lse, cosine, sine):
    return pl.pallas_call(
        attend_back_kernel,
        out_shape=jax.ShapeDtypeStruct((16, 3, 128, HEAD_DIM), bf16),
        in_specs=[smem_spec()] + [vmem_spec()] * 6,
        out_specs=vmem_spec(),
        scratch_shapes=[
            pltpu.VMEM((SEQ, HEAD_DIM), f32),
            pltpu.VMEM((SEQ, HEAD_DIM), f32),
            pltpu.VMEM((HEAD_DIM, SEQ), bf16),
        ],
        compiler_params=params(),
        cost_estimate=cost(15),
        name="attend_back",
    )(ends, qkv, grad, out, lse, cosine, sine)


PLANE = ("yl", "yh", "z")


def plane_exchange(value):
    return lax.all_to_all(value, PLANE, split_axis=0, concat_axis=0, tiled=True)


def rotary(count):
    places = jnp.arange(count, dtype=jnp.int32).astype(f32)
    within = jnp.arange(HEAD_DIM, dtype=jnp.int32) % (HEAD_DIM // 2)
    inverse_freq = 10000.0 ** (within.astype(f32) * (-2.0 / HEAD_DIM))
    angles = places[:, None] * inverse_freq[None, :]
    sign = jnp.where(jnp.arange(HEAD_DIM) < HEAD_DIM // 2, -1.0, 1.0).astype(f32)
    return jnp.cos(angles), jnp.sin(angles) * sign


def inverse_rms(values):
    return lax.rsqrt(jnp.mean(values * values, axis=-1, keepdims=True) + norm_eps)


def norm_back(grad_normed, values, inverse, gain):
    scaled = grad_normed * gain
    gain_part = jnp.sum(grad_normed * values * inverse, axis=0)
    inner = jnp.mean(scaled * values, axis=-1, keepdims=True)
    return inverse * scaled - values * inverse**3 * inner, gain_part


def on_device(
    tokens,
    block_lengths,
    attn_gain,
    query_weight,
    key_weight,
    value_weight,
    out_weight,
    mlp_gain,
    gate_weight,
    up_weight,
    down_weight,
    output_grad,
):
    x, yl, yh, z, c = (lax.axis_index(name) for name in ("x", "yl", "yh", "z", "c"))
    blk = (yh * 4 + z) * 2 + c
    rel = jnp.arange(16, dtype=jnp.int32)
    place = ((yh ^ ((rel >> 2) & 1)) * 4 + (z ^ (rel & 3))) * 2 + (c ^ (rel >> 3))
    chosen = place[:, None] == rel[None, :]

    def relative(gain):
        return jnp.sum(jnp.where(chosen[:, :, None], gain.reshape(1, 16, 128), 0.0), axis=1)

    def absolute(gain):
        return jnp.sum(jnp.where(chosen[:, :, None], gain.reshape(16, 1, 128), 0.0), axis=0)

    first_gain = relative(attn_gain).reshape(1, 2048)
    second_gain = relative(mlp_gain).reshape(1, 2048)
    cosine, sine = rotary(SEQ)
    own_cosine = lax.dynamic_slice_in_dim(cosine, blk * 128, 128, 0)
    own_sine = lax.dynamic_slice_in_dim(sine, blk * 128, 128, 0)
    sequence = (x ^ (blk >> 2)) * 2 + yl
    ends = jnp.cumsum(lax.dynamic_slice_in_dim(block_lengths, sequence, 1, 0)[0])

    normed1, tok, dy = prepare(place, tokens[0], output_grad[0], first_gain)
    tok = tok.astype(f32)
    blkaxes = ("yh", "z", "c")

    def exchange(value):
        return lax.all_to_all(value, blkaxes, split_axis=0, concat_axis=0, tiled=True)

    shard_a = jnp.concatenate([gate_weight.T, up_weight.T[:336]], axis=0)
    shard_b = jnp.concatenate([up_weight.T[336:], down_weight], axis=0)
    source = ((yl ^ (rel >> 3)) * 2 + (yh ^ ((rel >> 2) & 1))) * 4 + (z ^ (rel & 3))

    rows1 = gather4(normed1, "x")
    dy_rows = spread4(after(dy, rows1[4]), "x")
    mine = plane_exchange(share(query_weight, key_weight, value_weight, out_weight))
    mine = after(mine, *rows1[2:4], *dy_rows[1:], cosine, sine)
    w_attn = (mine, swap(mine, "c", 1))

    orders = "zy", "yz"
    shards = after(shard_a, mine), after(shard_b, mine)
    pieces = [spread4(v, o[0]) for v, o in zip(shards, orders)]
    qkv = project_qkv(source, rows1, w_attn, own_cosine, own_sine)
    qkv = exchange(after(qkv, *pieces[0], *pieces[1]))
    plane = [stacked(v) for v in pieces]
    low, attended, lse = attend(ends, after(qkv, *plane))
    low = exchange(low)
    near = [[swap(v, o[1], 1), swap(v, o[1], 3)] for v, o in zip(plane, orders)]
    part = project_out(source, after(low, *near[0], *near[1]), w_attn)
    residual = tok + scatter4([[part[k]] for k in range(4)], "x")
    groups = [gather_far(v, n, o[1]) for v, n, o in zip(plane, near, orders)]
    w_mlp = []
    for group in groups:
        held = [after(piece, residual) for piece in group]
        w_mlp += [*group, *(swap(piece, "c", 1) for piece in held)]
    inverse2 = inverse_rms(residual)
    normed2 = (residual * inverse2 * second_gain).astype(bf16)
    rows2 = gather4(normed2, "x")
    hidden, d_gate, d_up, part = mlp(rows2, dy_rows, w_mlp)

    far = scatter_far([part[2]], "x")
    near1, near3 = scatter_near([part[1]], [part[3]], far, "x")
    grads = mlp_grad(after(d_gate, *far), d_up, hidden, rows2, dy_rows)
    d_normed2 = add(part[0], after(near1, grads[0]), near3)
    back2, second_part = norm_back(d_normed2, residual, inverse2, second_gain)
    d_residual = dy.astype(f32) + back2
    d_attn = d_residual.astype(bf16)
    rows3 = gather4(d_attn, "x")

    orders = "yz", "zy"
    mine = grads[0], grads[2]
    got = [swap(after(v, d_attn), "c", 1) for v in (grads[1], grads[3])]
    terms = [pairs(m, g) for m, g in zip(mine, got)]
    sums = [far_sums(t[2]) for t in terms]
    rows3 = (after(rows3[0], *sums[0], *sums[1]),) + rows3[1:]
    far = [(swap(v[0], o[0], 1), swap(v[1], o[0], 3)) for v, o in zip(sums, orders)]
    d_out = out_back(source, rows3, w_attn)
    terms = [pairs(after(m, d_out), g) for m, g in zip(mine, got)]
    sums = [near_sums(t[1], t[3], f) for t, f in zip(terms, far)]
    d_out = exchange(d_out)
    d_out = after(d_out, *sums[0], *sums[1])
    near = [(swap(v[0], o[0], 1), swap(v[1], o[0], 3)) for v, o in zip(sums, orders)]
    dqkv = attend_back(ends, qkv, d_out, attended, lse, cosine, sine)
    dqkv = after(dqkv, *near[0], *near[1])
    down_part = project_down(after(hidden, dqkv), w_mlp)
    out_far = scatter_far([down_part[2]], "x")
    mine = after(mine[0], down_part), after(mine[1], down_part)
    terms = [pairs(m, g) for m, g in zip(mine, got)]
    along = [add(*t[0], *n).astype(bf16) for t, n in zip(terms, near)]
    dqkv = after(exchange(dqkv), *out_far, *along)

    qkv_mine, qkv_theirs = qkv_grad(dqkv, low, rows1, rows3)
    qkv_got = swap(qkv_theirs, "c", 1)
    part = qkv_back(source, after(dqkv, qkv_mine), w_attn)
    sums = far_sums(pairs(qkv_mine, qkv_got)[2])
    qkv_far = swap(sums[0], "z", 1), swap(sums[1], "z", 3)
    part = after(part, *sums)
    far = scatter_far([part[2]], "x")
    qkv_terms = pairs(after(qkv_mine, *far), qkv_got)
    sums = near_sums(qkv_terms[1], qkv_terms[3], qkv_far)
    qkv_near = swap(sums[0], "z", 1), swap(sums[1], "z", 3)
    d_near = scatter_near([part[1]], [part[3]], far, "x")
    d_normed1 = add(part[0], *d_near)
    out_near = scatter_near([after(down_part[1], *d_near)], [down_part[3]], out_far, "x")
    output = residual + add(down_part[0], *out_near)
    layer_output = restore(place, output.astype(bf16))[None]
    back1, first_part = norm_back(d_normed1, tok, inverse_rms(tok), first_gain)
    input_grad = d_residual + back1
    along = [after(v, *sums) for v in along]
    grad_a, grad_b = (
        collect4([[v[k]] for k in range(4)], o[1]) for v, o in zip(along, orders)
    )
    along = add(*qkv_terms[0], *qkv_near).astype(bf16)
    grad_qkv = collect4([[along[k]] for k in range(4)], "y")

    gains = jnp.concatenate([absolute(first_part), absolute(second_part)], axis=0)
    gains = total4(total4(gains, "x"), "y")
    gains = total4(after(gains, *qkv_near), "z")
    gains = gains + swap(gains, "c", 1)
    input_grad = restore(place, input_grad)[None]
    return (
        layer_output,
        input_grad,
        gains[:16].reshape(2048),
        grad_qkv[:256].T,
        grad_qkv[256:512].T,
        grad_qkv[512:768].T,
        grad_qkv[768:],
        gains[16:].reshape(2048),
        grad_a[:688].T,
        jnp.concatenate([grad_a[688:], grad_b[:352]], axis=0).T,
        grad_b[352:],
    )


def solution(mesh):
    fine = Mesh(mesh.devices.reshape(4, 2, 2, 4, 2), ("x", "yl", "yh", "z", "c"))
    head, blk = ("x", "yl"), ("yh", "z", "c")
    rows = P(head, blk, None)
    wide, tall = P(blk, head), P(head, blk)
    return jax.shard_map(
        on_device,
        mesh=fine,
        in_specs=(rows, P(), P(), wide, wide, wide, tall, P(), wide, wide, tall, rows),
        out_specs=(rows, rows, P(), wide, wide, wide, tall, P(), wide, wide, tall),
        check_vma=False,
    )
```
